32 devices in a mesh: section: 2 (over y), dp: 16 (over z, x, core).
Axes of the slice: x: 2, y: 2, z: 4, core: 2. Of those that a mesh axis runs over, the one named last changes fastest.
Arguments:
- images: bfloat16 [96, 196, 768], P('dp'), may hold values from -6 to 6
- cotangent: bfloat16 [96, 196, 768], P('dp'), may hold values from -6 to 6
- image_counts: int32 [16], P('dp'), may hold values from 1 to 6, 64 in all
- first_gain: float32 [2, 768], P('section'), may hold values from 0.1 to 1.9
- first_shift: float32 [2, 768], P('section'), may hold values from -1.5 to 1.5
- token_up: bfloat16 [2, 196, 384], P('section'), may hold values from -0.4375 to 0.4375
- token_bias: float32 [2, 384], P('section'), may hold values from -1.5 to 1.5
- token_down: bfloat16 [2, 384, 196], P('section'), may hold values from -0.3125 to 0.3125
- patch_bias: float32 [2, 196], P('section'), may hold values from -1.5 to 1.5
- second_gain: float32 [2, 768], P('section'), may hold values from 0.1 to 1.9
- second_shift: float32 [2, 768], P('section'), may hold values from -1.5 to 1.5
- channel_up: bfloat16 [2, 768, 3072], P('section'), may hold values from -0.21875 to 0.21875
- hidden_bias: float32 [2, 3072], P('section'), may hold values from -1.5 to 1.5
- channel_down: bfloat16 [2, 3072, 768], P('section'), may hold values from -0.109375 to 0.109375
- output_bias: float32 [2, 768], P('section'), may hold values from -1.5 to 1.5
Outputs:
- layer_outputs: bfloat16 [2, 96, 196, 768], P('section', 'dp')
- input_grads: bfloat16 [2, 96, 196, 768], P('section', 'dp')
- first_gain_grad: float32 [2, 768], P('section')
- first_shift_grad: float32 [2, 768], P('section')
- token_up_grad: float32 [2, 196, 384], P('section')
- token_bias_grad: float32 [2, 384], P('section')
- token_down_grad: float32 [2, 384, 196], P('section')
- patch_bias_grad: float32 [2, 196], P('section')
- second_gain_grad: float32 [2, 768], P('section')
- second_shift_grad: float32 [2, 768], P('section')
- channel_up_grad: float32 [2, 768, 3072], P('section')
- hidden_bias_grad: float32 [2, 3072], P('section')
- channel_down_grad: float32 [2, 3072, 768], P('section')
- output_bias_grad: float32 [2, 768], P('section')
The draws below stay inside these ranges and needn't reach their ends.
Inputs may be any that keep to these rules, and one draw needn't show every extreme that they name: `image_counts`: the live images of an index of dp are its first ones; the counts over all of dp sum to 64.
All inputs are finite; a program needn't handle non-finite values. No bound on the sum of `image_counts` on one device may be relied on, other than what follows from the above.
Results may differ from the reference program's by a relative error of at most 0.013.
Values may be sent and summed in bfloat16 or wider, within the bound.
No kernel may reach another device: no remote copies, remote signals or barrier semaphores. Data moves between devices by JAX's collectives and lax.ppermute only.
A program may use at most 256 MiB of HBM per device.

```python
import math
import jax
import jax.numpy as jnp
import numpy as np
from jax import lax

D = 768
TH = 384
FF = 3072
P_SIZE = 196
IMG_DEV = 6
IMAGES = 96
LIVE = 64
N_DP = 16


def shard_levels(key, shape, cuts, least, top_value):
    level = 1.0
    for dim, blocks in cuts:
        draws = jax.random.uniform(jax.random.fold_in(jax.random.fold_in(key, 6), dim), (blocks,), jnp.float32, least / len(cuts), top_value / len(cuts))
        level = level * jnp.repeat(jnp.exp(draws), shape[dim] // blocks).reshape((-1,) + (1,) * (len(shape) - 1 - dim))
    return level


def length_profile(count, total, reach, slope):
    weights = [(1 << 20) // math.isqrt(grade ** slope) + 1 for grade in range(2, count + 1)]
    surplus, holding = total - reach - (count - 1), [1] * (count - 1)
    while surplus > 0:
        candidates = [i for i in range(count - 1) if holding[i] < reach]
        pool, remaining = sum([weights[i] for i in candidates]), surplus
        for i in candidates:
            addition = min(reach - holding[i], max(1, remaining * weights[i] // pool), surplus)
            holding[i] = holding[i] + addition
            surplus = surplus - addition
    return np.array([reach] + holding)


def uneven_parts(rng, amount, total, bound, slope):
    if amount == 2:
        one = jax.random.randint(rng, (), max(1, total - bound), min(bound, total - 1) + 1)
        return jnp.stack([one, total - one])
    lengths = jnp.asarray(length_profile(amount, total, bound, slope), jnp.int32)
    twos = (amount - 1) // 2
    giver, receiver = lengths[1:1 + 2 * twos:2], lengths[2:2 + 2 * twos:2]
    margin = jnp.minimum(giver - 1, bound - receiver)
    moved = jax.random.randint(jax.random.fold_in(rng, 1), (twos,), 0, 1 << 20) % (margin + 1)
    lengths = lengths.at[1:1 + 2 * twos:2].set(giver - moved).at[2:2 + 2 * twos:2].set(receiver + moved)
    return lengths[jax.random.permutation(jax.random.fold_in(rng, 2), amount)]


def centred(stream_key, extent, deviation, most, split=(), kind=jnp.bfloat16):
    drawn = jax.random.normal(stream_key, extent, jnp.float32) * deviation
    if len(split) > 0:
        drawn = shard_levels(stream_key, extent, split, -0.22, 0.18) * drawn
    return jnp.clip(drawn, min=-most, max=most).astype(kind)


def setup_inputs(seed: int = 0) -> dict:
    seeds = jax.random.split(jax.random.key(seed), 16)
    return {
        "images": centred(seeds[0], (IMAGES, P_SIZE, D), 1.0, 6.0, ((0, 16),)),
        "cotangent": centred(seeds[1], (IMAGES, P_SIZE, D), 1.0, 6.0, ((0, 16),)),
        "image_counts": uneven_parts(seeds[2], N_DP, LIVE, IMG_DEV, 2).astype(jnp.int32),
        "first_gain": jnp.clip(1.0 + 0.18 * jax.random.normal(seeds[3], (2, D), jnp.float32), 0.1, 1.9),
        "first_shift": centred(seeds[4], (2, D), 0.3, 1.5, ((0, 2),), jnp.float32),
        "token_up": centred(seeds[5], (2, P_SIZE, TH), P_SIZE ** -0.5, 0.4375, ((0, 2),)),
        "token_bias": centred(seeds[6], (2, TH), 0.3, 1.5, ((0, 2),), jnp.float32),
        "token_down": centred(seeds[7], (2, TH, P_SIZE), TH ** -0.5, 0.3125, ((0, 2),)),
        "patch_bias": centred(seeds[8], (2, P_SIZE), 0.3, 1.5, ((0, 2),), jnp.float32),
        "second_gain": jnp.clip(1.0 + 0.18 * jax.random.normal(seeds[9], (2, D), jnp.float32), 0.1, 1.9),
        "second_shift": centred(seeds[10], (2, D), 0.3, 1.5, ((0, 2),), jnp.float32),
        "channel_up": centred(seeds[11], (2, D, FF), D ** -0.5, 0.21875, ((0, 2),)),
        "hidden_bias": centred(seeds[12], (2, FF), 0.3, 1.5, ((0, 2),), jnp.float32),
        "channel_down": centred(seeds[13], (2, FF, D), FF ** -0.5, 0.109375, ((0, 2),)),
        "output_bias": centred(seeds[14], (2, D), 0.3, 1.5, ((0, 2),), jnp.float32),
    }


@jax.custom_vjp
def low(v):
    return lax.optimization_barrier(v.astype(jnp.bfloat16)).astype(jnp.float32)

@jax.custom_vjp
def low_back(v):
    return v

def low_keep(v):
    return (low(v), None)

def low_pass(kept, grad):
    return (grad,)

def back_keep(v):
    return (v, None)

def back_low(kept, grad):
    return (low(grad),)
low.defvjp(low_keep, low_pass)
low_back.defvjp(back_keep, back_low)
EPS = 1e-06
PRECISE = lax.Precision.HIGHEST

def normalize(stream, scaling, offset):
    center = stream - lax.optimization_barrier(jnp.mean(stream, axis=-1, keepdims=True))
    spread = lax.optimization_barrier(jnp.mean(center * center, axis=-1, keepdims=True))
    return center * lax.rsqrt(spread + EPS) * scaling + offset

def mixer_layer(stream, params, live_rows):
    first_gain, first_shift, token_up, token_bias, token_down, patch_bias, second_gain, second_shift, channel_up, hidden_bias, channel_down, output_bias = params
    normed = low(normalize(stream, first_gain, first_shift))
    token_pre = low_back(jnp.einsum('npd,pk->ndk', normed, token_up, precision=PRECISE) + token_bias)
    token_act = low(jax.nn.gelu(token_pre, approximate=False))
    token_mix = low_back(jnp.einsum('ndk,kp->npd', token_act, token_down, precision=PRECISE) + patch_bias[:, None])
    middle = stream + token_mix
    renormed = low(normalize(middle, second_gain, second_shift))
    channel_pre = low_back(jnp.einsum('npd,df->npf', renormed, channel_up, precision=PRECISE) + hidden_bias)
    channel_act = low(jax.nn.gelu(channel_pre, approximate=False))
    channel_mix = low_back(jnp.einsum('npf,fd->npd', channel_act, channel_down, precision=PRECISE) + output_bias)
    return (middle + channel_mix) * live_rows[:, None, None]

def two_layers(inputs, nudging, layer_zero, layer_one, live_slots):

    def step(unused, pieces):
        images_block, nudge_block, live_block = pieces
        hidden = mixer_layer(images_block, layer_zero, live_block)
        passed = low_back(low(hidden) + nudge_block)
        final = mixer_layer(passed, layer_one, live_block)
        return (unused, (final, hidden))
    unused, (finals, hiddens) = lax.scan(jax.checkpoint(step), jnp.zeros((), jnp.float32), (inputs, nudging, live_slots))
    return (finals, hiddens)

def reference(images, cotangent, image_counts, first_gain, first_shift, token_up, token_bias, token_down, patch_bias, second_gain, second_shift, channel_up, hidden_bias, channel_down, output_bias):
    live_slots = (jnp.arange(IMG_DEV, dtype=jnp.int32)[None, :] < image_counts[:, None]).astype(jnp.float32)
    weights = tuple((w.astype(jnp.float32) for w in (first_gain, first_shift, token_up, token_bias, token_down, patch_bias, second_gain, second_shift, channel_up, hidden_bias, channel_down, output_bias)))
    layer_zero = tuple((w[0] for w in weights))
    layer_one = tuple((w[1] for w in weights))
    inputs = images.astype(jnp.float32).reshape(N_DP, IMG_DEV, P_SIZE, D)
    nudging = jnp.zeros((N_DP, IMG_DEV, P_SIZE, D), jnp.float32)

    def forward_all(inputs, nudging, layer_zero, layer_one):
        return two_layers(inputs, nudging, layer_zero, layer_one, live_slots)
    finals, pullback, hiddens = jax.vjp(forward_all, inputs, nudging, layer_zero, layer_one, has_aux=True)
    seed_grad = cotangent.astype(jnp.float32).reshape(N_DP, IMG_DEV, P_SIZE, D)
    input_grad, hidden_grad, zero_grads, one_grads = pullback(seed_grad)
    layer_outputs = jnp.stack([hiddens.reshape(IMAGES, P_SIZE, D), finals.reshape(IMAGES, P_SIZE, D)]).astype(jnp.bfloat16)
    input_grads = jnp.stack([input_grad.reshape(IMAGES, P_SIZE, D), hidden_grad.reshape(IMAGES, P_SIZE, D)]).astype(jnp.bfloat16)
    return (layer_outputs, input_grads, jnp.stack([zero_grads[0], one_grads[0]]), jnp.stack([zero_grads[1], one_grads[1]]), jnp.stack([zero_grads[2], one_grads[2]]), jnp.stack([zero_grads[3], one_grads[3]]), jnp.stack([zero_grads[4], one_grads[4]]), jnp.stack([zero_grads[5], one_grads[5]]), jnp.stack([zero_grads[6], one_grads[6]]), jnp.stack([zero_grads[7], one_grads[7]]), jnp.stack([zero_grads[8], one_grads[8]]), jnp.stack([zero_grads[9], one_grads[9]]), jnp.stack([zero_grads[10], one_grads[10]]), jnp.stack([zero_grads[11], one_grads[11]]))
```

```python
import functools
import math

import jax
import jax.numpy as jnp
from jax import lax
from jax.experimental import pallas as pl
from jax.experimental.pallas import tpu as pltpu
from jax.sharding import PartitionSpec as P

EPS = 1e-06
BF, F32 = jnp.bfloat16, jnp.float32
HALF_ROOT = math.sqrt(0.5)
PEAK = 1.0 / math.sqrt(2.0 * math.pi)
FB = 256
VMEM_LIMIT = 40 << 20
RING = 8

ANY = pl.BlockSpec(memory_space=pl.ANY)
VM = pl.BlockSpec(memory_space=pltpu.VMEM)
SM = pl.BlockSpec(memory_space=pltpu.SMEM)

TU0, TD0, FG0, FS0, SG0, SS0, OB0, HB0, TB0, PB0, TROWS = 0, 200, 400, 402, 404, 406, 408, 416, 424, 432, 512

KEPT_FORWARD = ("act", "ren", "normed", "tact", "out", "gp", "tgp", "mid")
KEPT_BOTH = ("act", "ren", "normed", "tact", "out", "og", "pg", "mix", "tpg", "ing", "tab")
KEPT_BACK = ("og", "pg", "ing", "tab")
ZERO_WIDE = ("act", "ren", "og", "pg")
ZERO_OUT = ("out", "ing")


def nn(a, b):
    return jnp.dot(a, b, preferred_element_type=F32)


def nt(a, b):
    return lax.dot_general(a, b, (((1,), (1,)), ((), ())), preferred_element_type=F32)


def tn(a, b):
    return lax.dot_general(a, b, (((0,), (0,)), ((), ())), preferred_element_type=F32)


def padded(rows):
    return -(-rows // 16) * 16


def gelu_parts(z):
    u = z * HALF_ROOT
    phi = 0.5 + 0.5 * lax.erf(u)
    slope = phi + (z * PEAK) * jnp.exp(-(u * u))
    return (z * phi).astype(BF), slope.astype(BF)


def standardize(v):
    center = v - jnp.mean(v, axis=-1, keepdims=True)
    spread = jnp.mean(center * center, axis=-1, keepdims=True)
    inverse = lax.rsqrt(spread + EPS)
    return center * inverse, inverse


def norm_back(y, xhat, inverse):
    return (
        y - jnp.mean(y, axis=-1, keepdims=True) - xhat * jnp.mean(y * xhat, axis=-1, keepdims=True)
    ) * inverse


def rows_sum(v):
    return jnp.sum(v, axis=0, keepdims=True)


def add_row(tab, row, vec):
    width = tab.shape[1]
    for i in range(vec.shape[1] // width):
        tab[row + i : row + i + 1, :] += vec[:, i * width : (i + 1) * width]


def column(row):
    return jnp.transpose(jnp.broadcast_to(row, (8, row.shape[1])))[:, 0:1]


def shapes_of(slots, p, d, ff, th):
    q = padded(p)
    return dict(
        act=((slots, q, ff), BF),
        ren=((slots, q, d), BF),
        og=((slots, q, d), BF),
        pg=((slots, q, ff), BF),
        gp=((slots, p, ff), BF),
        normed=((slots, p, d), BF),
        tact=((slots, th, d), BF),
        tgp=((slots, th, d), BF),
        tpg=((slots, th, d), BF),
        mix=((slots, p, d), BF),
        mid=((slots, p, d), F32),
        out=((slots, p, d), BF),
        ing=((slots, p, d), BF),
        tab=((TROWS, th), F32),
    )


def forward_slot(v, i, p, w):
    xh, _ = standardize(v["x"][i].astype(F32))
    normed = (xh * w["g1"][...] + w["b1"][...]).astype(BF)
    v["normed"][i] = normed
    act, slope = gelu_parts(nn(w["tuT"][...], normed) + column(w["tb"][...]))
    v["tact"][i] = act
    v["tgp"][i] = slope
    v["mid"][i] = v["x"][i].astype(F32) + (nn(w["tdT"][...], act) + column(w["pb"][...]))
    xh2, _ = standardize(v["mid"][i])
    v["ren"][i, 0:p] = (xh2 * w["g2"][...] + w["b2"][...]).astype(BF)
    ff = w["w1"].shape[1]
    cuts = [slice(j, j + FB) for j in range(0, ff, FB)]
    pre = nn(v["ren"][i, 0:p], w["w1"][:, cuts[0]])
    total = None
    for j, cut in enumerate(cuts):
        ahead = nn(v["ren"][i, 0:p], w["w1"][:, cuts[j + 1]]) if j + 1 < len(cuts) else None
        if j > 0:
            part = nn(v["act"][i, 0:p, cuts[j - 1]], w["w2"][cuts[j - 1], :])
            total = part if total is None else total + part
        act, slope = gelu_parts(pre + w["hb"][:, cut])
        v["act"][i, 0:p, cut] = act
        v["gp"][i, :, cut] = slope
        pre = ahead
    total = total + nn(v["act"][i, 0:p, cuts[-1]], w["w2"][cuts[-1], :])
    v["out"][i] = (v["mid"][i] + (total + w["ob"][...])).astype(BF)


def back_slot(v, i, p, w, tab):
    og = v["cot"][i]
    v["og"][i, 0:p] = og
    ff = w["w1T"].shape[0]
    width = tab.shape[1]
    cuts = [slice(j, j + FB) for j in range(0, ff, FB)]
    act_grad = nn(og, w["w2T"][:, cuts[0]])
    norm_grad = None
    for j, cut in enumerate(cuts):
        ahead = nn(og, w["w2T"][:, cuts[j + 1]]) if j + 1 < len(cuts) else None
        if j > 0:
            part = nn(v["pg"][i, 0:p, cuts[j - 1]], w["w1T"][cuts[j - 1], :])
            norm_grad = part if norm_grad is None else norm_grad + part
        pre_grad = act_grad * v["gp"][i, :, cut].astype(F32)
        v["pg"][i, 0:p, cut] = pre_grad.astype(BF)
        sums = rows_sum(pre_grad)
        for k in range(0, FB, 128):
            c, o = divmod(j * FB + k, width)
            tab[HB0 + c : HB0 + c + 1, o : o + 128] += sums[:, k : k + 128]
        act_grad = ahead
    norm_grad = norm_grad + nn(v["pg"][i, 0:p, cuts[-1]], w["w1T"][cuts[-1], :])
    xh2, inv2 = standardize(v["mid"][i])
    live = og.astype(F32)
    add_row(tab, OB0, rows_sum(live))
    add_row(tab, SG0, rows_sum(norm_grad * xh2))
    add_row(tab, SS0, rows_sum(norm_grad))
    middle_grad = live + norm_back(w["g2"][...] * norm_grad, xh2, inv2)
    mix = middle_grad.astype(BF)
    v["mix"][i] = mix
    tpg = (nn(w["td"][...], mix) * v["tgp"][i].astype(F32)).astype(BF)
    v["tpg"][i] = tpg
    first_grad = nn(w["tu"][...], tpg)
    xh, inv = standardize(v["x"][i].astype(F32))
    add_row(tab, FG0, rows_sum(first_grad * xh))
    add_row(tab, FS0, rows_sum(first_grad))
    v["ing"][i] = (middle_grad + norm_back(w["g1"][...] * first_grad, xh, inv)).astype(BF)


def token_slot(v, i, p, tab):
    ones = jnp.ones((8, v["mix"].shape[-1]), BF)
    tab[TB0 : TB0 + 8, :] += nt(ones, v["tpg"][i])
    tab[PB0 : PB0 + 8, 0:p] += nt(ones, v["mix"][i])
    tab[TU0 : TU0 + p, :] += nt(v["normed"][i], v["tpg"][i])
    tab[TD0 : TD0 + p, :] += nt(v["mix"][i], v["tact"][i])


def stage_kernel(plan, *refs):
    mode, lo, m, p = plan["mode"], plan["lo"], plan["m"], plan["p"]
    it = iter(refs)
    sc = next(it)
    ins = {name: next(it) for name in plan["ins"]}
    w = {name: next(it) for name in plan["weights"]}
    for _ in range(plan["threaded"]):
        next(it)
    outs = {name: next(it) for name in plan["outs"]}
    send = next(it) if plan["send"] else None
    v = {name: next(it) for name in plan["buffers"]}
    tab = next(it) if "tab" in outs else None
    zero, blank_out = (next(it), next(it)) if plan["zeros"] else (None, None)
    for name in plan["turned"]:
        w[name + "T"] = next(it)
    in_sem, out_sem, tab_sem = next(it), next(it), next(it)

    mine = sc[1] == plan["flag"]
    live = jnp.where(mine, jnp.clip(sc[0] - lo, 0, m), 0)

    def in_copies(i):
        return [
            pltpu.make_async_copy(ins[name].at[base + i], v[name].at[i], in_sem.at[k, i])
            for k, (name, base) in enumerate(plan["bases"].items())
        ]

    def out_copy(name, i):
        k = plan["moved"].index(name)
        return pltpu.make_async_copy(v[name].at[i], outs[name].at[lo + i], out_sem.at[k, i])

    def send_copy(i):
        name = "ing" if mode == "both" else "out"
        return pltpu.make_async_copy(v[name].at[i], send.at[i], out_sem.at[len(plan["moved"]), i])

    def zero_copy(name, i):
        k = plan["moved"].index(name)
        source = blank_out if name in ZERO_OUT else zero.at[:, 0 : v[name].shape[-1]]
        return pltpu.make_async_copy(source, outs[name].at[lo + i], out_sem.at[k, i])

    def each(wanted, action):
        for i in range(m):
            pl.when(wanted(i))(functools.partial(action, i))

    def start_all(copies):
        for c in copies:
            c.start()

    def wait_all(copies):
        for c in copies:
            c.wait()

    @pl.when(live > 0)
    def _():
        each(lambda i: i < live, lambda i: start_all(in_copies(i)))
        if tab is not None:
            pltpu.make_async_copy(outs["tab"], tab, tab_sem).start()
        for name in plan["turned"]:
            w[name + "T"][...] = jnp.transpose(w[name][...].astype(F32)).astype(BF)
        for name in ZERO_WIDE:
            if name in v:
                for i in range(m):
                    v[name][i, p:, :] = jnp.zeros((v[name].shape[1] - p, v[name].shape[2]), BF)
        if tab is not None:
            pltpu.make_async_copy(outs["tab"], tab, tab_sem).wait()

    blank = jnp.logical_and(mine, live < m)
    if plan["zeros"]:
        @pl.when(blank)
        def _():
            zero[...] = jnp.zeros_like(zero)
            blank_out[...] = jnp.zeros_like(blank_out)
            each(lambda i: i >= live, lambda i: start_all([zero_copy(n, i) for n in plan["zeros"]]))

    late = [n for n in plan["moved"] if n in ("og", "pg", "mix", "tpg", "ing")]
    early = [n for n in plan["moved"] if n not in late]

    def slot(i, carry):
        wait_all(in_copies(i))
        if mode != "back":
            forward_slot(v, i, p, w)
            start_all([out_copy(n, i) for n in early])
            if mode == "forward":
                send_copy(i).start()
        if mode != "forward":
            back_slot(v, i, p, w, tab)
            if mode == "both":
                send_copy(i).start()
            start_all([out_copy(n, i) for n in late])
            if mode == "back":
                token_slot(v, i, p, tab)
        return carry

    lax.fori_loop(0, live, slot, 0)

    @pl.when(live > 0)
    def _():
        if tab is not None:
            c = pltpu.make_async_copy(tab, outs["tab"], tab_sem)
            c.start()
            c.wait()
        each(lambda i: i < live, lambda i: wait_all([out_copy(n, i) for n in plan["moved"]]))
        if send is not None:
            each(lambda i: i < live, lambda i: send_copy(i).wait())

    if plan["zeros"]:
        @pl.when(blank)
        def _():
            each(lambda i: i >= live, lambda i: wait_all([zero_copy(n, i) for n in plan["zeros"]]))


def stage(mode, lo, m, sizes, sc, weights, kept, ins):
    slots, p, d, ff, th = sizes
    shapes = shapes_of(*sizes)
    names = {"forward": KEPT_FORWARD, "both": KEPT_BOTH, "back": KEPT_BACK}[mode]
    moved = [n for n in names if n != "tab"]
    zeros = [n for n in names if n in ZERO_WIDE + ZERO_OUT] if lo + m > 1 else []
    keys = {
        "forward": ["g1", "b1", "tu", "tb", "td", "pb", "g2", "b2", "hb", "ob", "w1", "w2"],
        "both": ["g1", "b1", "tu", "tb", "td", "pb", "g2", "b2", "hb", "ob", "w1", "w2", "w1T", "w2T"],
        "back": ["g1", "tu", "td", "g2", "w1T", "w2T"],
    }[mode]
    turned = [] if mode == "back" else ["tu", "td"]
    buffers = {
        "forward": ["x"] + moved,
        "both": ["x", "cot"] + moved + ["gp", "tgp", "mid"],
        "back": ["x", "cot", "gp", "tgp", "mid", "normed", "tact", "mix", "tpg"] + moved,
    }[mode]
    threaded = [n for n in names if n in kept]
    bases = {n: b for n, (_, b) in ins.items()}
    shapes.update(x=((slots, p, d), BF), cot=((slots, p, d), BF))

    args = [sc] + [a for a, _ in ins.values()] + [weights[k] for k in keys]
    specs = [SM] + [ANY] * len(ins) + [VM] * len(keys)
    aliases = {len(args) + k: names.index(n) for k, n in enumerate(threaded)}
    args += [kept[n] for n in threaded]
    specs += [ANY] * len(threaded)
    out_shape = [jax.ShapeDtypeStruct(*shapes[n]) for n in names]
    send = mode != "back"
    if send:
        out_shape.append(jax.ShapeDtypeStruct((m, p, d), BF))
    scratch = [pltpu.VMEM((m,) + shapes[n][0][1:], shapes[n][1]) for n in buffers]
    if "tab" in names:
        scratch.append(pltpu.VMEM(*shapes["tab"]))
    if zeros:
        scratch += [pltpu.VMEM((padded(p), ff), BF), pltpu.VMEM((p, d), BF)]
    for n in turned:
        scratch.append(pltpu.VMEM(weights[n].shape[::-1], BF))
    scratch += [
        pltpu.SemaphoreType.DMA((len(ins), m)),
        pltpu.SemaphoreType.DMA((len(moved) + 1, m)),
        pltpu.SemaphoreType.DMA,
    ]
    plan = dict(
        mode=mode, lo=lo, m=m, p=p, flag=0 if mode == "both" else 1, ins=list(ins), weights=keys,
        threaded=len(threaded), outs=list(names), send=send, buffers=buffers, moved=moved, zeros=zeros,
        turned=turned, bases=bases,
    )
    unit = 2 * p * d * 2 * (ff + th) * m
    outs = pl.pallas_call(
        functools.partial(stage_kernel, plan),
        out_shape=out_shape,
        in_specs=specs,
        out_specs=[ANY] * len(out_shape),
        scratch_shapes=scratch,
        input_output_aliases=aliases,
        compiler_params=pltpu.CompilerParams(vmem_limit_bytes=VMEM_LIMIT),
        cost_estimate=pl.CostEstimate(
            flops=unit * (2 if mode == "both" else 1), bytes_accessed=4 << 20, transcendentals=0
        ),
        name=f"{mode}_{lo}",
    )(*args)
    new = dict(kept)
    new.update(zip(names, outs))
    return new, (outs[-1] if send else None)


def token_kernel(p, sc, normed_in, tact_in, mix_in, tpg_in, old, tab_out, normed, tact, mix, tpg, tab, sems, tab_sem):
    live = jnp.where(sc[1] == 0, sc[0], 0)
    pairs = ((normed_in, normed), (tact_in, tact), (mix_in, mix), (tpg_in, tpg))

    def copies(i):
        return [pltpu.make_async_copy(a.at[i], b.at[i], sems.at[k, i]) for k, (a, b) in enumerate(pairs)]

    @pl.when(live > 0)
    def _():
        c = pltpu.make_async_copy(tab_out, tab, tab_sem)
        c.start()

        def begin(i, carry):
            for one in copies(i):
                one.start()
            return carry

        lax.fori_loop(0, live, begin, 0)
        c.wait()

        def work(i, carry):
            for one in copies(i):
                one.wait()
            token_slot(dict(normed=normed, tact=tact, mix=mix, tpg=tpg), i, p, tab)
            return carry

        lax.fori_loop(0, live, work, 0)
        c = pltpu.make_async_copy(tab, tab_out, tab_sem)
        c.start()
        c.wait()


def token_grads(sizes, sc, kept):
    slots, p = sizes[:2]
    names = ("normed", "tact", "mix", "tpg")
    shapes = shapes_of(*sizes)
    return pl.pallas_call(
        functools.partial(token_kernel, p),
        out_shape=jax.ShapeDtypeStruct(*shapes["tab"]),
        in_specs=[SM] + [ANY] * 5,
        out_specs=ANY,
        scratch_shapes=[pltpu.VMEM(*shapes[n]) for n in names]
        + [pltpu.VMEM(*shapes["tab"]), pltpu.SemaphoreType.DMA((4, slots)), pltpu.SemaphoreType.DMA],
        input_output_aliases={5: 0},
        compiler_params=pltpu.CompilerParams(vmem_limit_bytes=VMEM_LIMIT),
        name="token_grads",
    )(sc, *[kept[n] for n in names], kept["tab"])


def down_grads(act, og):
    rows, ff = act.shape
    d = og.shape[1]
    wide = 512

    def kernel(a, g, o):
        o[...] = tn(a[...], g[...]).astype(BF)

    return pl.pallas_call(
        kernel,
        grid=(ff // wide,),
        out_shape=jax.ShapeDtypeStruct((ff, d), BF),
        in_specs=[pl.BlockSpec((rows, wide), lambda j: (0, j)), pl.BlockSpec((rows, d), lambda j: (0, 0))],
        out_specs=pl.BlockSpec((wide, d), lambda j: (j, 0)),
        compiler_params=pltpu.CompilerParams(vmem_limit_bytes=VMEM_LIMIT),
        cost_estimate=pl.CostEstimate(flops=2 * rows * ff * d, bytes_accessed=16 << 20, transcendentals=0),
        name="down_grads",
    )(act, og)


def up_grads(ren, pg, tab):
    rows, d = ren.shape
    ff = pg.shape[1]
    each = ff // RING
    small = tab.shape[0] // (2 * RING)
    half = d // 2

    def kernel(r, g, t, o):
        for k in range(2):
            full = tn(r[...], g[:, k * each : (k + 1) * each])
            for h in range(2):
                o[h, k, 0:half, :] = full[h * half : (h + 1) * half].astype(BF)
                o[h, k, half:, :] = t[h, k].astype(BF)

    return pl.pallas_call(
        kernel,
        grid=(RING // 2,),
        out_shape=jax.ShapeDtypeStruct((2, RING, half + small, each), BF),
        in_specs=[
            pl.BlockSpec((rows, d), lambda j: (0, 0)),
            pl.BlockSpec((rows, 2 * each), lambda j: (0, j)),
            pl.BlockSpec((2, 2, small, each), lambda j: (0, j, 0, 0)),
        ],
        out_specs=pl.BlockSpec((2, 2, half + small, each), lambda j: (0, j, 0, 0)),
        compiler_params=pltpu.CompilerParams(vmem_limit_bytes=VMEM_LIMIT),
        cost_estimate=pl.CostEstimate(flops=2 * rows * ff * d, bytes_accessed=16 << 20, transcendentals=0),
        name="up_grads",
    )(ren, pg, tab.reshape(2, RING, small, each))


def ring_sums(parts, count):
    chips = count // 2
    order = [c for c in range(chips) if c % 2 == 0] + [c for c in range(chips) if c % 2 == 1][::-1]
    place = {c: i for i, c in enumerate(order)}
    forward = [(2 * c, 2 * order[(place[c] + 1) % chips]) for c in range(chips)]
    backward = [(2 * c + 1, 2 * order[(place[c] - 1) % chips] + 1) for c in range(chips)]
    ring = forward + backward
    swap = [(i, i ^ 1) for i in range(count)]
    index = lax.axis_index("dp")
    core = index % 2
    spots = jnp.array([place[i // 2] if i % 2 == 0 else chips - 1 - place[i // 2] for i in range(count)], jnp.int32)
    me = spots[index]

    def chunk(array, k):
        return lax.dynamic_index_in_dim(array, k % chips, 0, keepdims=False)

    held = []
    for part in parts:
        other = lax.dynamic_index_in_dim(part, 1 - core, 0, keepdims=False)
        own = lax.dynamic_index_in_dim(part, core, 0, keepdims=False)
        held.append(own + lax.ppermute(other, "dp", swap))
    moving = [chunk(a, me + chips - 1) for a in held]
    for step in range(chips - 1):
        arrived = [lax.ppermute(c, "dp", ring) for c in moving]
        moving = [r + chunk(a, me + 2 * chips - 2 - step) for r, a in zip(arrived, held)]
    totals = [[c] for c in moving]
    for step in range(chips - 1):
        moving = [lax.ppermute(c, "dp", ring) for c in moving]
        for t, c in zip(totals, moving):
            t.append(c)
    results = []
    for t, a in zip(totals, held):
        mine = jnp.zeros_like(a)
        for step, c in enumerate(t):
            mine = lax.dynamic_update_index_in_dim(mine, c, (me + 2 * chips - step) % chips, 0)
        theirs = lax.ppermute(mine, "dp", swap)
        results.append((jnp.where(core == 0, mine, theirs), jnp.where(core == 0, theirs, mine)))
    return results


def body(images, cotangent, image_counts, first_gain, first_shift, token_up, token_bias, token_down, patch_bias,
         second_gain, second_shift, channel_up, hidden_bias, channel_down, output_bias):
    slots, p, d = images.shape
    ff, th = channel_up.shape[2], token_up.shape[2]
    sizes = (slots, p, d, ff, th)
    count = lax.axis_size("dp")
    leading = lax.axis_index("section") == 0
    sc = jnp.concatenate([image_counts, leading.astype(jnp.int32)[None]])
    weights = dict(
        g1=first_gain, b1=first_shift, tu=token_up[0], tb=token_bias, td=token_down[0], pb=patch_bias,
        g2=second_gain, b2=second_shift, w1=channel_up[0], hb=hidden_bias, w2=channel_down[0], ob=output_bias,
    )
    cuts = [(0, 1)] + [(lo, min(2, slots - 1 - lo)) for lo in range(1, slots - 1, 2)] + [(slots - 1, 1)]

    kept, sent = {}, []
    for lo, m in cuts:
        kept, out = stage("forward", lo, m, sizes, sc, weights, kept, {"x": (images, lo)})
        sent.append(lax.ppermute(out, "section", [(0, 1)]))
    w1, w2, kept["act"] = lax.optimization_barrier((weights["w1"], weights["w2"], kept["act"]))
    weights["w1T"], weights["w2T"] = jnp.transpose(w1), jnp.transpose(w2)
    kept["tab"] = jnp.zeros((TROWS, th), F32)

    def back(number):
        nonlocal kept
        lo, m = cuts[number]
        ins = {"x": (images, lo), "cot": (returned[number], 0)}
        ins.update({n: (kept[n], lo) for n in ("gp", "tgp", "mid", "normed", "tact")})
        kept, _ = stage("back", lo, m, sizes, sc, weights, kept, ins)

    returned = []
    for number, (lo, m) in enumerate(cuts):
        kept, grad = stage(
            "both", lo, m, sizes, sc, weights, kept, {"x": (sent[number], 0), "cot": (cotangent, lo)}
        )
        returned.append(lax.ppermute(grad, "section", [(1, 0)]))
        if number >= 1:
            back(number - 1)
    back(len(cuts) - 1)

    flat = {n: kept[n].reshape(-1, kept[n].shape[-1]) for n in ("act", "ren", "og", "pg")}
    down = down_grads(flat["act"], flat["og"])
    tab = token_grads(sizes, sc, kept)
    up = up_grads(flat["ren"], flat["pg"], tab)
    down = down.reshape(2, RING, ff // (2 * RING), d)
    if count == 2 * RING:
        (down_a, down_b), (up_a, up_b) = ring_sums([down, up], count)
    else:
        down_sum, up_sum = lax.psum((down.astype(F32), up.astype(F32)), "dp")
        (down_a, down_b), (up_a, up_b) = (down_sum[0], down_sum[1]), (up_sum[0], up_sum[1])
    down_sum = jnp.stack([down_a, down_b]).astype(F32).reshape(1, ff, d)
    half = d // 2
    up_sum = jnp.stack([up_a[:, :half], up_b[:, :half]]).astype(F32)
    up_sum = up_sum.transpose(0, 2, 1, 3).reshape(1, d, ff)
    tab = jnp.stack([up_a[:, half:], up_b[:, half:]]).astype(F32).reshape(TROWS, th)

    def vector(row, length):
        rows = -(-length // th)
        return tab[row : row + rows].reshape(1, rows * th)[:, :length]

    return (
        kept["out"][None],
        kept["ing"][None],
        vector(FG0, d),
        vector(FS0, d),
        tab[TU0 : TU0 + p][None],
        vector(TB0, th),
        tab[TD0 : TD0 + p].T[None],
        vector(PB0, p),
        vector(SG0, d),
        vector(SS0, d),
        up_sum,
        vector(HB0, ff),
        down_sum,
        vector(OB0, d),
    )


def solution(mesh):
    row = P("section", None)
    mat = P("section", None, None)
    in_specs = (
        P("dp", None, None), P("dp", None, None), P("dp"), row, row, mat, row, mat, row, row, row, mat, row, mat, row,
    )
    stream = P("section", "dp", None, None)
    out_specs = (stream, stream, row, row, mat, row, mat, row, row, row, mat, row, mat, row)
    return jax.shard_map(body, mesh=mesh, in_specs=in_specs, out_specs=out_specs, check_vma=False)
```

```python
import functools
import math

import jax
import jax.numpy as jnp
from jax import lax
from jax.experimental import pallas as pl
from jax.experimental.pallas import tpu as pltpu
from jax.sharding import PartitionSpec as P

EPS = 1e-06
BF, F32 = jnp.bfloat16, jnp.float32
HALF_ROOT = math.sqrt(0.5)
PEAK = 1.0 / math.sqrt(2.0 * math.pi)
FB = 512
VMEM_LIMIT = 63 << 20
RING = 8
FINISH = ((0, 8),)

ANY = pl.BlockSpec(memory_space=pltpu.HBM)
FREE = pl.BlockSpec(memory_space=pl.ANY)
VM = pl.BlockSpec(memory_space=pltpu.VMEM)
SM = pl.BlockSpec(memory_space=pltpu.SMEM)
TINY = pl.CostEstimate(flops=1 << 10, bytes_accessed=1 << 10, transcendentals=0)

TU0, TD0, FG0, FS0, SG0, SS0, OB0, HB0, TB0, PB0, TROWS = 0, 200, 400, 402, 404, 406, 408, 416, 424, 432, 512

KEPT_FORWARD = ("act", "ren", "normed", "tact", "out", "gp", "tgp", "mid")
KEPT_BOTH = ("act", "ren", "normed", "tact", "out", "og", "pg", "mix", "tpg", "ing", "tab")
KEPT_BACK = ("og", "pg", "ing", "tab")
ZERO_WIDE = ("act", "ren", "og", "pg")
ZERO_OUT = ("out", "ing")


def nn(a, b):
    return jnp.dot(a, b, preferred_element_type=F32)


def nt(a, b):
    return lax.dot_general(a, b, (((1,), (1,)), ((), ())), preferred_element_type=F32)


def tn(a, b):
    return lax.dot_general(a, b, (((0,), (0,)), ((), ())), preferred_element_type=F32)


def padded(rows):
    return -(-rows // 16) * 16


def gelu_parts(z):
    u = z * HALF_ROOT
    phi = 0.5 + 0.5 * lax.erf(u)
    slope = phi + (z * PEAK) * jnp.exp(-(u * u))
    return (z * phi).astype(BF), slope.astype(BF)


def standardize(v):
    center = v - jnp.mean(v, axis=-1, keepdims=True)
    spread = jnp.mean(center * center, axis=-1, keepdims=True)
    inverse = lax.rsqrt(spread + EPS)
    return center * inverse, inverse


def norm_back(y, xhat, inverse):
    return (
        y - jnp.mean(y, axis=-1, keepdims=True) - xhat * jnp.mean(y * xhat, axis=-1, keepdims=True)
    ) * inverse


def rows_sum(v):
    return jnp.sum(v, axis=0, keepdims=True)


def add_row(tab, row, vec):
    width = tab.shape[1]
    for i in range(vec.shape[1] // width):
        tab[row + i : row + i + 1, :] += vec[:, i * width : (i + 1) * width]


def column(row):
    return jnp.transpose(jnp.broadcast_to(row, (8, row.shape[1])))[:, 0:1]


def shapes_of(slots, p, d, ff, th):
    q = padded(p)
    return dict(
        act=((slots, q, ff), BF),
        ren=((slots, q, d), BF),
        og=((slots, q, d), BF),
        pg=((slots, q, ff), BF),
        gp=((slots, p, ff), BF),
        normed=((slots, p, d), BF),
        tact=((slots, th, d), BF),
        tgp=((slots, th, d), BF),
        tpg=((slots, th, d), BF),
        mix=((slots, p, d), BF),
        mid=((slots, p, d), F32),
        out=((slots, p, d), BF),
        ing=((slots, p, d), BF),
        tab=((TROWS, th), F32),
    )


def forward_token(v, x, p, w):
    xh, _ = standardize(x)
    normed = (xh * w["g1"][...] + w["b1"][...]).astype(BF)
    v["normed"][...] = normed
    act, slope = gelu_parts(nn(w["tuT"][...], normed) + column(w["tb"][...]))
    v["tact"][...] = act
    v["tgp"][...] = slope
    v["mid"][...] = x + (nn(w["tdT"][...], act) + column(w["pb"][...]))
    xh2, _ = standardize(v["mid"][...])
    v["ren"][0:p] = (xh2 * w["g2"][...] + w["b2"][...]).astype(BF)


def forward_channel(v, p, w):
    ff = w["w1"].shape[1]
    cuts = [slice(j, j + FB) for j in range(0, ff, FB)]
    pre = nn(v["ren"][0:p], w["w1"][:, cuts[0]])
    total = None
    for j, cut in enumerate(cuts):
        ahead = nn(v["ren"][0:p], w["w1"][:, cuts[j + 1]]) if j + 1 < len(cuts) else None
        if j > 0:
            part = nn(v["act"][0:p, cuts[j - 1]], w["w2"][cuts[j - 1], :])
            total = part if total is None else total + part
        act, slope = gelu_parts(pre + w["hb"][:, cut])
        v["act"][0:p, cut] = act
        v["gp"][:, cut] = slope
        pre = ahead
    total = total + nn(v["act"][0:p, cuts[-1]], w["w2"][cuts[-1], :])
    v["out"][...] = (v["mid"][...] + (total + w["ob"][...])).astype(BF)


def back_slot(v, x, og, p, w, tab):
    v["og"][0:p] = og
    ff = v["pg"].shape[1]
    width = tab.shape[1]

    def through_down(cut):
        return nn(og, w["w2T"][:, cut]) if "w2T" in w else nt(og, w["w2"][cut, :])

    def through_up(cut):
        pre_grad = v["pg"][0:p, cut]
        return nn(pre_grad, w["w1T"][cut, :]) if "w1T" in w else nt(pre_grad, w["w1"][:, cut])

    cuts = [slice(j, j + FB) for j in range(0, ff, FB)]
    act_grad = through_down(cuts[0])
    norm_grad = None
    for j, cut in enumerate(cuts):
        ahead = through_down(cuts[j + 1]) if j + 1 < len(cuts) else None
        if j > 0:
            part = through_up(cuts[j - 1])
            norm_grad = part if norm_grad is None else norm_grad + part
        pre_grad = act_grad * v["gp"][:, cut].astype(F32)
        v["pg"][0:p, cut] = pre_grad.astype(BF)
        sums = rows_sum(pre_grad)
        for k in range(0, FB, 128):
            c, o = divmod(j * FB + k, width)
            tab[HB0 + c : HB0 + c + 1, o : o + 128] += sums[:, k : k + 128]
        act_grad = ahead
    norm_grad = norm_grad + through_up(cuts[-1])
    xh2, inv2 = standardize(v["mid"][...])
    live = og.astype(F32)
    add_row(tab, OB0, rows_sum(live))
    add_row(tab, SG0, rows_sum(norm_grad * xh2))
    add_row(tab, SS0, rows_sum(norm_grad))
    middle_grad = live + norm_back(w["g2"][...] * norm_grad, xh2, inv2)
    mix = middle_grad.astype(BF)
    v["mix"][...] = mix
    tpg = (nn(w["td"][...], mix) * v["tgp"][...].astype(F32)).astype(BF)
    v["tpg"][...] = tpg
    first_grad = nn(w["tu"][...], tpg)
    xh, inv = standardize(x)
    add_row(tab, FG0, rows_sum(first_grad * xh))
    add_row(tab, FS0, rows_sum(first_grad))
    v["ing"][...] = (middle_grad + norm_back(w["g1"][...] * first_grad, xh, inv)).astype(BF)


def token_slot(normed, tact, mix, tpg, p, tab):
    ones = jnp.ones((8, mix.shape[-1]), BF)
    tab[TB0 : TB0 + 8, :] += nt(ones, tpg)
    tab[PB0 : PB0 + 8, 0:p] += nt(ones, mix)
    tab[TU0 : TU0 + p, :] += nt(normed, tpg)
    tab[TD0 : TD0 + p, :] += nt(mix, tact)


GROUP_TOKEN = ("normed", "tact", "tgp", "mid", "ren")
GROUP_CHANNEL = ("act", "gp", "out")
GROUP_BACK = ("og", "pg", "mix", "tpg", "ing")


def stage_kernel(plan, *refs):
    mode, lo, m, p = plan["mode"], plan["lo"], plan["m"], plan["p"]
    it = iter(refs)
    sc = next(it)
    ins = {name: [next(it) for _ in range(parts)] for name, parts in plan["ins"].items()}
    sources = {name: next(it) for name in plan["weights"]}
    for _ in range(plan["threaded"]):
        next(it)
    outs = {name: next(it) for name in plan["outs"]}
    send = [next(it) for _ in range(m)] if plan["send"] else None
    v = {name: next(it) for name in plan["buffers"]}
    tab = next(it) if "tab" in outs else None
    zero, blank_out = (next(it), next(it)) if plan["zeros"] else (None, None)
    w = {name: next(it) for name in plan["weights"]}
    for name in plan["turned"]:
        w[name] = next(it)
    in_sem, out_sem, tab_sem, load_sem = next(it), next(it), next(it), next(it)

    mine = sc[1] == plan["flag"]
    live = jnp.where(mine, jnp.clip(sc[0] - lo, 0, m), 0)
    moved = plan["moved"]

    def load(name):
        return pltpu.make_async_copy(sources[name], w[name], load_sem.at[plan["weights"].index(name)])

    def in_copies(i):
        return [
            pltpu.make_async_copy(refs[i] if plan["single"][name] else refs[0].at[lo + i], v[name].at[i], in_sem.at[k, i])
            for k, (name, refs) in enumerate(ins.items())
        ]

    def out_copies(names, i):
        return [
            pltpu.make_async_copy(v[name], outs[name].at[lo + i], out_sem.at[moved.index(name)])
            for name in names
            if name in moved
        ]

    def send_copy(i):
        return pltpu.make_async_copy(v[plan["send"]], send[i], out_sem.at[len(moved)])

    def switch(i, action):
        for k in range(m):
            pl.when(i == k)(functools.partial(action, k))

    def zero_copy(name, i):
        source = blank_out if name in ZERO_OUT else zero.at[:, 0 : v[name].shape[-1]]
        return pltpu.make_async_copy(source, outs[name].at[lo + i], tab_sem.at[1])

    def start_all(copies):
        for c in copies:
            c.start()

    def wait_all(copies):
        for c in copies:
            c.wait()

    def first_wait(i, names):
        @pl.when(i == 0)
        def _():
            wait_all([load(name) for name in names])

    def free(i, group):
        @pl.when(i > 0)
        def _():
            wait_all(out_copies(group, i - 1))
            if send is not None and plan["send"] in group:
                send_copy(0).wait()

    blank = jnp.logical_and(mine, live < m)
    if plan["zeros"]:
        @pl.when(blank)
        def _():
            zero[...] = jnp.zeros_like(zero)
            blank_out[...] = jnp.zeros_like(blank_out)
            for i in range(m):
                @pl.when(i >= live)
                def _():
                    start_all([zero_copy(n, i) for n in plan["zeros"]])

    small = [n for n in plan["weights"] if n not in LARGE]

    @pl.when(live > 0)
    def _():
        for i in range(m):
            @pl.when(i < live)
            def _():
                start_all(in_copies(i))
        for name in plan["weights"]:
            if name in small:
                load(name).start()
        if tab is not None:
            pltpu.make_async_copy(outs["tab"], tab, tab_sem.at[0]).start()
        for name in plan["weights"]:
            if name in LARGE:
                load(name).start()
        for name in ZERO_WIDE:
            if name in v:
                v[name][p:, :] = jnp.zeros((v[name].shape[0] - p, v[name].shape[1]), BF)
        wait_all([load(name) for name in small])
        for name, source in plan["turned"].items():
            w[name][...] = jnp.transpose(w[source][...].astype(F32)).astype(BF)
        if tab is not None:
            pltpu.make_async_copy(outs["tab"], tab, tab_sem.at[0]).wait()

    def slot(i, carry):
        switch(i, lambda k: wait_all(in_copies(k)))
        x = v["x"][i].astype(F32)
        if mode != "back":
            free(i, GROUP_TOKEN)
            forward_token(v, x, p, w)
            start_all(out_copies(GROUP_TOKEN, i))
            first_wait(i, ("w1", "w2"))
            free(i, GROUP_CHANNEL)
            forward_channel(v, p, w)
            if mode == "forward":
                switch(i, lambda k: send_copy(k).start())
            start_all(out_copies(GROUP_CHANNEL, i))
        if mode != "forward":
            first_wait(i, ("w2T", "w1T") if mode == "both" else ("w2", "w1"))
            free(i, GROUP_BACK)
            kept = v if mode == "both" else {**v, **{n: v[n].at[i] for n in ("gp", "tgp", "mid", "normed", "tact")}}
            back_slot(kept, x, v["cot"][i], p, w, tab)
            if mode == "both":
                switch(i, lambda k: send_copy(k).start())
            start_all(out_copies(GROUP_BACK, i))
            if mode == "back":
                token_slot(kept["normed"][...], kept["tact"][...], v["mix"][...], v["tpg"][...], p, tab)
        return carry

    lax.fori_loop(0, live, slot, 0)

    @pl.when(live > 0)
    def _():
        if tab is not None:
            c = pltpu.make_async_copy(tab, outs["tab"], tab_sem.at[0])
            c.start()
            c.wait()
        wait_all(out_copies(GROUP_TOKEN + GROUP_CHANNEL + GROUP_BACK, live - 1))
        if send is not None:
            send_copy(0).wait()

    if plan["zeros"]:
        @pl.when(blank)
        def _():
            for i in range(m):
                @pl.when(i >= live)
                def _():
                    wait_all([zero_copy(n, i) for n in plan["zeros"]])


LARGE = ("w1", "w2", "w1T", "w2T")


def stage(mode, lo, m, sizes, sc, weights, kept, ins):
    slots, p, d, ff, th = sizes
    shapes = shapes_of(*sizes)
    names = {"forward": KEPT_FORWARD, "both": KEPT_BOTH, "back": KEPT_BACK}[mode]
    moved = [n for n in names if n != "tab"]
    zeros = [n for n in names if n in ZERO_WIDE + ZERO_OUT] if lo + m > 1 else []
    keys = {
        "forward": ["g1", "b1", "tu", "tb", "tdT", "pb", "g2", "b2", "hb", "ob", "w1", "w2"],
        "both": ["g1", "b1", "tu", "tb", "tdT", "pb", "g2", "b2", "hb", "ob", "w1", "w2", "w1T", "w2T"],
        "back": ["g1", "tu", "tdT", "g2", "w1", "w2"],
    }[mode]
    turned = {"forward": {"tuT": "tu"}, "both": {"tuT": "tu", "td": "tdT"}, "back": {"td": "tdT"}}[mode]
    buffers = {
        "forward": ["x"] + moved,
        "both": ["x", "cot"] + moved + ["gp", "tgp", "mid"],
        "back": ["x", "cot", "gp", "tgp", "mid", "normed", "tact", "mix", "tpg"] + moved,
    }[mode]
    threaded = [n for n in names if n in kept]
    single = {n: isinstance(a, list) for n, a in ins.items()}
    ins = {n: a if single[n] else [a] for n, a in ins.items()}
    shapes.update(x=((slots, p, d), BF), cot=((slots, p, d), BF))

    given = [a for arrays in ins.values() for a in arrays]
    args = [sc] + given + [weights[k] for k in keys]
    specs = [SM] + [FREE if single[n] else ANY for n, arrays in ins.items() for _ in arrays] + [ANY] * len(keys)
    aliases = {len(args) + k: names.index(n) for k, n in enumerate(threaded)}
    args += [kept[n] for n in threaded]
    specs += [ANY] * len(threaded)
    out_shape = [jax.ShapeDtypeStruct(*shapes[n]) for n in names]
    send = mode != "back"
    if send:
        out_shape += [jax.ShapeDtypeStruct((p, d), BF)] * m
    scratch = [
        pltpu.VMEM(((m,) if n in ins else ()) + shapes[n][0][1:], shapes[n][1]) for n in buffers
    ]
    if "tab" in names:
        scratch.append(pltpu.VMEM(*shapes["tab"]))
    if zeros:
        scratch += [pltpu.VMEM((padded(p), ff), BF), pltpu.VMEM((p, d), BF)]
    scratch += [pltpu.VMEM(weights[k].shape, weights[k].dtype) for k in keys]
    scratch += [pltpu.VMEM(weights[n].shape[::-1], BF) for n in turned.values()]
    scratch += [
        pltpu.SemaphoreType.DMA((len(ins), m)),
        pltpu.SemaphoreType.DMA((len(moved) + 1,)),
        pltpu.SemaphoreType.DMA((2,)),
        pltpu.SemaphoreType.DMA((len(keys),)),
    ]
    plan = dict(
        mode=mode, lo=lo, m=m, p=p, flag=0 if mode == "both" else 1, ins={n: len(a) for n, a in ins.items()}, weights=keys,
        threaded=len(threaded), outs=list(names), send={"forward": "out", "both": "ing", "back": None}[mode],
        buffers=buffers, moved=moved, zeros=zeros, turned=turned, single=single,
    )
    outs = pl.pallas_call(
        functools.partial(stage_kernel, plan),
        out_shape=out_shape,
        in_specs=specs,
        out_specs=[ANY] * len(out_shape),
        scratch_shapes=scratch,
        input_output_aliases=aliases,
        compiler_params=pltpu.CompilerParams(vmem_limit_bytes=VMEM_LIMIT),
        cost_estimate=TINY,
        name=f"{mode}_{lo}",
    )(*args)
    new = dict(kept)
    new.update(zip(names, outs))
    return new, (list(outs[-m:]) if send else None)


def token_kernel(p, sc, normed_in, tact_in, mix_in, tpg_in, old, tab_out, normed, tact, mix, tpg, tab, sems, tab_sem):
    live = jnp.where(sc[1] == 0, sc[0], 0)
    pairs = ((normed_in, normed), (tact_in, tact), (mix_in, mix), (tpg_in, tpg))

    def copies(i):
        return [pltpu.make_async_copy(a.at[i], b.at[i], sems.at[k, i]) for k, (a, b) in enumerate(pairs)]

    @pl.when(live > 0)
    def _():
        c = pltpu.make_async_copy(tab_out, tab, tab_sem)
        c.start()

        def begin(i, carry):
            for one in copies(i):
                one.start()
            return carry

        lax.fori_loop(0, live, begin, 0)
        c.wait()

        def work(i, carry):
            for one in copies(i):
                one.wait()
            token_slot(normed[i], tact[i], mix[i], tpg[i], p, tab)
            return carry

        lax.fori_loop(0, live, work, 0)
        c = pltpu.make_async_copy(tab, tab_out, tab_sem)
        c.start()
        c.wait()


def token_grads(sizes, sc, kept):
    slots, p = sizes[:2]
    names = ("normed", "tact", "mix", "tpg")
    shapes = shapes_of(*sizes)
    return pl.pallas_call(
        functools.partial(token_kernel, p),
        out_shape=jax.ShapeDtypeStruct(*shapes["tab"]),
        in_specs=[SM] + [ANY] * 5,
        out_specs=ANY,
        scratch_shapes=[pltpu.VMEM(*shapes[n]) for n in names]
        + [pltpu.VMEM(*shapes["tab"]), pltpu.SemaphoreType.DMA((4, slots)), pltpu.SemaphoreType.DMA],
        input_output_aliases={5: 0},
        compiler_params=pltpu.CompilerParams(vmem_limit_bytes=VMEM_LIMIT),
        cost_estimate=TINY,
        name="token_grads",
    )(sc, *[kept[n] for n in names], kept["tab"])


def turned_kernel(sc, w1, w2, w1T, w2T, a, b, at, bt, in_sem, out_sem):
    ff = w1.shape[1]
    wide = 512
    blocks = ff // wide

    def ins(j):
        cut = pl.ds(j * wide, wide)
        return [
            pltpu.make_async_copy(w1.at[:, cut], a.at[:, cut], in_sem.at[0, j]),
            pltpu.make_async_copy(w2.at[cut], b.at[cut], in_sem.at[1, j]),
        ]

    def outs(j):
        cut = pl.ds(j * wide, wide)
        return [
            pltpu.make_async_copy(at.at[cut], w1T.at[cut], out_sem.at[0, j]),
            pltpu.make_async_copy(bt.at[:, cut], w2T.at[:, cut], out_sem.at[1, j]),
        ]

    @pl.when(sc[1] == 0)
    def _():
        for j in range(blocks):
            for c in ins(j):
                c.start()
        for j in range(blocks):
            for c in ins(j):
                c.wait()
            cut = slice(j * wide, (j + 1) * wide)
            at[cut, :] = jnp.transpose(a[:, cut])
            bt[:, cut] = jnp.transpose(b[cut, :])
            for c in outs(j):
                c.start()
        for j in range(blocks):
            for c in outs(j):
                c.wait()


def turned_weights(sc, w1, w2):
    d, ff = w1.shape
    blocks = ff // 512
    return pl.pallas_call(
        turned_kernel,
        out_shape=[jax.ShapeDtypeStruct((ff, d), BF), jax.ShapeDtypeStruct((d, ff), BF)],
        in_specs=[SM, ANY, ANY],
        out_specs=[ANY, ANY],
        scratch_shapes=[
            pltpu.VMEM((d, ff), BF), pltpu.VMEM((ff, d), BF), pltpu.VMEM((ff, d), BF), pltpu.VMEM((d, ff), BF),
            pltpu.SemaphoreType.DMA((2, blocks)), pltpu.SemaphoreType.DMA((2, blocks)),
        ],
        compiler_params=pltpu.CompilerParams(vmem_limit_bytes=VMEM_LIMIT),
        cost_estimate=TINY,
        name="turned_weights",
    )(sc, w1, w2)


def split_halves(core, full, own, other):
    half = full.shape[1] // 2
    left, right = full[:, :half].astype(BF), full[:, half:].astype(BF)

    @pl.when(core == 0)
    def _():
        own[...] = left
        other[...] = right

    @pl.when(core != 0)
    def _():
        own[...] = right
        other[...] = left


def down_grads(core, act, og):
    rows, ff = act.shape
    d = og.shape[1]
    each = ff // RING

    def kernel(c, a, g, own, other):
        for k in range(2):
            split_halves(c[0], tn(a[:, k * each : (k + 1) * each], g[...]), own.at[k], other.at[k])

    shape = jax.ShapeDtypeStruct((RING, each, d // 2), BF)
    block = pl.BlockSpec((2, each, d // 2), lambda j: (j, 0, 0))
    return pl.pallas_call(
        kernel,
        grid=(RING // 2,),
        out_shape=[shape, shape],
        in_specs=[
            SM,
            pl.BlockSpec((rows, 2 * each), lambda j: (0, j)),
            pl.BlockSpec((rows, d), lambda j: (0, 0)),
        ],
        out_specs=[block, block],
        compiler_params=pltpu.CompilerParams(vmem_limit_bytes=VMEM_LIMIT),
        cost_estimate=TINY,
        name="down_grads",
    )(core, act, og)


def up_grads(core, ren, pg, tab):
    rows, d = ren.shape
    ff = pg.shape[1]
    each = ff // RING
    half = d // 2
    small = tab.shape[0] // (2 * RING)

    def kernel(c, r, g, t, own, other):
        full = tn(r[...], g[...])
        for k in range(2):
            part = full[:, k * each : (k + 1) * each]
            top = jnp.concatenate([part[:half], t[0, k]], axis=0).astype(BF)
            low = jnp.concatenate([part[half:], t[1, k]], axis=0).astype(BF)

            @pl.when(c[0] == 0)
            def _():
                own[k] = top
                other[k] = low

            @pl.when(c[0] != 0)
            def _():
                own[k] = low
                other[k] = top

    shape = jax.ShapeDtypeStruct((RING, half + small, each), BF)
    block = pl.BlockSpec((2, half + small, each), lambda j: (j, 0, 0))
    return pl.pallas_call(
        kernel,
        grid=(RING // 2,),
        out_shape=[shape, shape],
        in_specs=[
            SM,
            pl.BlockSpec((rows, d), lambda j: (0, 0)),
            pl.BlockSpec((rows, 2 * each), lambda j: (0, j)),
            pl.BlockSpec((2, 2, small, each), lambda j: (0, j, 0, 0)),
        ],
        out_specs=[block, block],
        compiler_params=pltpu.CompilerParams(vmem_limit_bytes=VMEM_LIMIT),
        cost_estimate=TINY,
        name="up_grads",
    )(core, ren, pg, tab.reshape(2, RING, small, each))


def ring_plan(count):
    chips = count // 2
    order = [c for c in range(chips) if c % 2 == 0] + [c for c in range(chips) if c % 2 == 1][::-1]
    place = {c: i for i, c in enumerate(order)}
    forward = [(2 * c, 2 * order[(place[c] + 1) % chips]) for c in range(chips)]
    backward = [(2 * c + 1, 2 * order[(place[c] - 1) % chips] + 1) for c in range(chips)]
    spots = [place[i // 2] if i % 2 == 0 else chips - 1 - place[i // 2] for i in range(count)]
    return forward + backward, spots


def ring_sums(parts, count):
    chips = count // 2
    ring, spots = ring_plan(count)
    swap = [(i, i ^ 1) for i in range(count)]
    me = jnp.array(spots, jnp.int32)[lax.axis_index("dp")]

    def chunk(pair, k):
        return sum(lax.dynamic_index_in_dim(a, k % chips, 0, keepdims=False) for a in pair)

    held = [(own, lax.ppermute(other, "dp", swap)) for own, other in parts]
    moving = [chunk(a, me + chips - 1) for a in held]
    for step in range(chips - 1):
        arrived = [lax.ppermute(c, "dp", ring) for c in moving]
        moving = [r + chunk(a, me + 2 * chips - 2 - step) for r, a in zip(arrived, held)]
    mine, theirs = [[c] for c in moving], [[lax.ppermute(c, "dp", swap)] for c in moving]
    for step in range(chips - 1):
        if step > 0:
            for i, c in enumerate(moving):
                moving[i], theirs[i][-2 if step > 1 else -1] = lax.optimization_barrier(
                    (c, theirs[i][-2 if step > 1 else -1])
                )
        moving = [lax.ppermute(c, "dp", ring) for c in moving]
        for i, c in enumerate(moving):
            mine[i].append(c)
            theirs[i].append(lax.ppermute(c, "dp", swap))
    return mine, theirs


def finish_kernel(p, first, last, threaded, *refs):
    it = iter(refs)
    where = next(it)
    steps = range(first, last)
    chunks = [[{s: next(it) for s in steps} for _ in range(2)] for _ in range(2)]
    for _ in range(threaded):
        next(it)
    down, up, tab_out = next(it), next(it), next(it)
    final = last == RING
    if final:
        fg, fs, tu, tb, td, pb, sg, ss, hb, ob = [next(it) for _ in range(10)]
    taken = [next(it), next(it)]
    given = [next(it), next(it)]
    tab = next(it)
    in_sem, out_sem, tab_sem = next(it), next(it), next(it)
    each = down.shape[1] // RING
    half = down.shape[2] // 2
    small = taken[1].shape[1] - half
    jobs = [(kind, side, s) for s in steps for side in range(2) for kind in range(2)]
    depth = taken[0].shape[0]

    def place(side, s):
        at = where[side] + 2 * RING - s
        return lax.rem(at, RING), (where[2] if side == 0 else 1 - where[2])

    def fetch(n):
        kind, side, s = jobs[n]
        slot = n // 2 % depth
        return pltpu.make_async_copy(chunks[kind][side][s], taken[kind].at[slot], in_sem.at[kind, slot])

    def store(n):
        kind, side, s = jobs[n]
        k, h = place(side, s)
        slot = n // 2 % depth
        by_ff = pl.ds(pl.multiple_of(k * each, each), each)
        by_half = pl.ds(pl.multiple_of(h * half, half), half)
        target = down.at[0, by_ff, by_half] if kind == 0 else up.at[0, by_half, by_ff]
        return pltpu.make_async_copy(given[kind].at[slot], target, out_sem.at[kind, slot])

    def old_table():
        return pltpu.make_async_copy(tab_out, tab, tab_sem)

    lag = 2 * depth
    if first > 0:
        old_table().start()
    for n in range(min(lag, len(jobs))):
        fetch(n).start()
    if first > 0:
        old_table().wait()
    for n, (kind, side, s) in enumerate(jobs):
        fetch(n).wait()
        if n >= lag:
            store(n - lag).wait()
        slot = n // 2 % depth
        given[kind][slot] = taken[kind][slot, 0:half].astype(F32)
        store(n).start()
        if kind == 1:
            k, h = place(side, s)
            tab[pl.ds(pl.multiple_of((h * RING + k) * small, small), small), :] = taken[1][slot, half:].astype(F32)
        if n + lag < len(jobs):
            fetch(n + lag).start()
    keep = pltpu.make_async_copy(tab, tab_out, tab_sem)
    keep.start()

    def vector(ref, row):
        width = tab.shape[1]
        length = ref.shape[1]
        for i in range(-(-length // width)):
            size = min(width, length - i * width)
            ref[:, i * width : i * width + size] = tab[row + i : row + i + 1, 0:size]

    if final:
        tu[:, 0, :] = tab[TU0 : TU0 + p, :]
        td[:, 0, :] = tab[TD0 : TD0 + p, :]
        for ref, row in ((fg, FG0), (fs, FS0), (tb, TB0), (pb, PB0), (sg, SG0), (ss, SS0), (hb, HB0), (ob, OB0)):
            vector(ref, row)
    for n in range(max(0, len(jobs) - lag), len(jobs)):
        store(n).wait()
    keep.wait()


def finish(where, mine, theirs, sizes):
    slots, p, d, ff, th = sizes
    half, each = d // 2, ff // RING
    rows = mine[1][0].shape[0]
    big = [jax.ShapeDtypeStruct(s, F32) for s in ((1, ff, d), (1, d, ff), (TROWS, th))]
    few = [
        jax.ShapeDtypeStruct(s, F32)
        for s in ((1, d), (1, d), (p, 1, th), (1, th), (p, 1, th), (1, p), (1, d), (1, d), (1, ff), (1, d))
    ]
    depth = 4
    scratch = [pltpu.VMEM((depth, half, each), BF), pltpu.VMEM((depth, rows, each), BF)]
    scratch += [pltpu.VMEM((depth, half, each), F32), pltpu.VMEM((depth, half, each), F32)]
    scratch += [
        pltpu.VMEM((TROWS, th), F32), pltpu.SemaphoreType.DMA((2, depth)), pltpu.SemaphoreType.DMA((2, depth)),
        pltpu.SemaphoreType.DMA,
    ]
    results = []
    for first, last in FINISH:
        args = [side[kind][s] for kind in range(2) for side in (mine, theirs) for s in range(first, last)]
        aliases = {1 + len(args) + i: i for i in range(len(results))}
        final = last == RING
        out = pl.pallas_call(
            functools.partial(finish_kernel, p, first, last, len(results)),
            out_shape=big + (few if final else []),
            in_specs=[SM] + [FREE] * len(args) + [ANY] * len(results),
            out_specs=[ANY] * 3 + ([VM] * len(few) if final else []),
            scratch_shapes=scratch,
            input_output_aliases=aliases,
            compiler_params=pltpu.CompilerParams(vmem_limit_bytes=VMEM_LIMIT),
            cost_estimate=pl.CostEstimate(
                flops=1 << 10, bytes_accessed=(last - first) * (4 << 20), transcendentals=0
            ),
            name=f"finish_{first}",
        )(where, *args, *results)
        results = list(out[:3])
    fg, fs, tu, tb, td, pb, sg, ss, hb, ob = out[3:]
    down, up = results[:2]
    return down, up, fg, fs, tu.transpose(1, 0, 2), tb, td.transpose(1, 2, 0), pb, sg, ss, hb, ob


def body(images, cotangent, image_counts, first_gain, first_shift, token_up, token_bias, token_down, patch_bias,
         second_gain, second_shift, channel_up, hidden_bias, channel_down, output_bias):
    slots, p, d = images.shape
    ff, th = channel_up.shape[2], token_up.shape[2]
    sizes = (slots, p, d, ff, th)
    count = lax.axis_size("dp")
    leading = lax.axis_index("section") == 0
    sc = jnp.concatenate([image_counts, leading.astype(jnp.int32)[None]])
    weights = dict(
        g1=first_gain, b1=first_shift, tu=token_up[0], tb=token_bias, tdT=token_down[0].T, pb=patch_bias,
        g2=second_gain, b2=second_shift, w1=channel_up[0], hb=hidden_bias, w2=channel_down[0], ob=output_bias,
    )
    cuts = [(0, 1)] + [(lo, min(2, slots - 1 - lo)) for lo in range(1, slots - 1, 2)] + [(slots - 1, 1)]

    kept, sent, returned = {}, [], []

    def forward(number):
        nonlocal kept
        lo, m = cuts[number]
        kept, out = stage("forward", lo, m, sizes, sc, weights, kept, {"x": images})
        sent.append([lax.ppermute(o, "section", [(0, 1)]) for o in out])

    def both(number):
        nonlocal kept
        lo, m = cuts[number]
        ins = {"x": sent[number], "cot": cotangent}
        kept, grad = stage("both", lo, m, sizes, sc, weights, kept, ins)
        returned.append([lax.ppermute(g, "section", [(1, 0)]) for g in grad])

    def back(number):
        nonlocal kept
        lo, m = cuts[number]
        ins = {"x": images, "cot": returned[number]}
        ins.update({n: kept[n] for n in ("gp", "tgp", "mid", "normed", "tact")})
        kept, _ = stage("back", lo, m, sizes, sc, weights, kept, ins)

    last = len(cuts) - 1
    forward(0)
    forward(1)
    w1, w2, kept["act"] = lax.optimization_barrier((weights["w1"], weights["w2"], kept["act"]))
    weights["w1T"], weights["w2T"] = turned_weights(sc, w1, w2)
    kept["tab"] = jnp.zeros((TROWS, th), F32)
    assert last >= 2
    for number in range(last + 1):
        if number >= 2:
            back(number - 2)
        both(number)
        if number + 2 <= last:
            forward(number + 2)
    back(last - 1)
    back(last)

    flat = {n: kept[n].reshape(-1, kept[n].shape[-1]) for n in ("act", "ren", "og", "pg")}
    index = lax.axis_index("dp")
    core = (index % 2).astype(jnp.int32)
    half, each = d // 2, ff // RING
    down = down_grads(core[None], flat["act"], flat["og"])
    tab = token_grads(sizes, sc, kept)
    up = up_grads(core[None], flat["ren"], flat["pg"], tab)
    if count == 2 * RING:
        mine, theirs = ring_sums([down, up], count)
        spots = jnp.array(ring_plan(count)[1], jnp.int32)
        where = jnp.stack([spots[index], spots[index ^ 1], core])
    else:
        whole = [jnp.where(core == 0, jnp.stack(pair), jnp.stack(pair[::-1])) for pair in (down, up)]
        whole = [w.astype(BF) for w in lax.psum([w.astype(F32) for w in whole], "dp")]
        mine = [[w[0, -s % RING] for s in range(RING)] for w in whole]
        theirs = [[w[1, -s % RING] for s in range(RING)] for w in whole]
        where = jnp.zeros((3,), jnp.int32)
    grads = finish(where, mine, theirs, sizes)
    down_sum, up_sum, fg, fs, tu, tb, td, pb, sg, ss, hb, ob = grads
    return (kept["out"][None], kept["ing"][None], fg, fs, tu, tb, td, pb, sg, ss, up_sum, hb, down_sum, ob)


def solution(mesh):
    row = P("section", None)
    mat = P("section", None, None)
    in_specs = (
        P("dp", None, None), P("dp", None, None), P("dp"), row, row, mat, row, mat, row, row, row, mat, row, mat, row,
    )
    stream = P("section", "dp", None, None)
    out_specs = (stream, stream, row, row, mat, row, mat, row, row, row, mat, row, mat, row)
    return jax.shard_map(body, mesh=mesh, in_specs=in_specs, out_specs=out_specs, check_vma=False)
```

```python
import functools
import math

import jax
import jax.numpy as jnp
from jax import lax
from jax.experimental import pallas as pl
from jax.experimental.pallas import tpu as pltpu
from jax.sharding import PartitionSpec as P

EPS = 1e-06
BF, F32 = jnp.bfloat16, jnp.float32
HALF_ROOT = math.sqrt(0.5)
PEAK = 1.0 / math.sqrt(2.0 * math.pi)
FB, BB = 1024, 512
VMEM_LIMIT = 63 << 20
RING = 8
FINISH = ((0, 8),)

ANY = pl.BlockSpec(memory_space=pltpu.HBM)
FREE = pl.BlockSpec(memory_space=pl.ANY)
VM = pl.BlockSpec(memory_space=pltpu.VMEM)
SM = pl.BlockSpec(memory_space=pltpu.SMEM)
TINY = pl.CostEstimate(flops=1 << 10, bytes_accessed=1 << 10, transcendentals=0)

TU0, TD0, FG0, FS0, SG0, SS0, OB0, HB0, TB0, PB0, TROWS = 0, 200, 400, 402, 404, 406, 408, 416, 424, 432, 512

KEPT_FORWARD = ("act", "ren", "normed", "tact", "out", "gp", "tgp", "mid")
KEPT_BOTH = ("act", "ren", "normed", "tact", "out", "og", "pg", "mix", "tpg", "ing", "tab")
KEPT_BACK = ("og", "pg", "ing", "tab")
ZERO_WIDE = ("act", "ren", "og", "pg")
ZERO_OUT = ("out", "ing")


def nn(a, b):
    return jnp.dot(a, b, preferred_element_type=F32)


def nt(a, b):
    return lax.dot_general(a, b, (((1,), (1,)), ((), ())), preferred_element_type=F32)


def tn(a, b):
    return lax.dot_general(a, b, (((0,), (0,)), ((), ())), preferred_element_type=F32)


def padded(rows):
    return -(-rows // 16) * 16


def gelu_parts(z):
    u = z * HALF_ROOT
    phi = 0.5 + 0.5 * lax.erf(u)
    slope = phi + (z * PEAK) * jnp.exp(-(u * u))
    return (z * phi).astype(BF), slope.astype(BF)


def standardize(v):
    center = v - jnp.mean(v, axis=-1, keepdims=True)
    spread = jnp.mean(center * center, axis=-1, keepdims=True)
    inverse = lax.rsqrt(spread + EPS)
    return center * inverse, inverse


def norm_back(y, xhat, inverse):
    return (
        y - jnp.mean(y, axis=-1, keepdims=True) - xhat * jnp.mean(y * xhat, axis=-1, keepdims=True)
    ) * inverse


def rows_sum(v):
    return jnp.sum(v, axis=0, keepdims=True)


def add_row(tab, row, vec):
    width = tab.shape[1]
    for i in range(vec.shape[1] // width):
        tab[row + i : row + i + 1, :] += vec[:, i * width : (i + 1) * width]


def column(row):
    return jnp.transpose(jnp.broadcast_to(row, (8, row.shape[1])))[:, 0:1]


def shapes_of(slots, p, d, ff, th):
    q = padded(p)
    return dict(
        act=((slots, q, ff), BF),
        ren=((slots, q, d), BF),
        og=((slots, q, d), BF),
        pg=((slots, q, ff), BF),
        gp=((slots, p, ff), BF),
        normed=((slots, p, d), BF),
        tact=((slots, th, d), BF),
        tgp=((slots, th, d), BF),
        tpg=((slots, th, d), BF),
        mix=((slots, p, d), BF),
        mid=((slots, p, d), F32),
        out=((slots, p, d), BF),
        ing=((slots, p, d), BF),
        tab=((TROWS, th), F32),
    )


def forward_token(v, x, p, w):
    xh, _ = standardize(x)
    normed = (xh * w["g1"][...] + w["b1"][...]).astype(BF)
    v["normed"][...] = normed
    act, slope = gelu_parts(nn(w["tuT"][...], normed) + column(w["tb"][...]))
    v["tact"][...] = act
    v["tgp"][...] = slope
    v["mid"][...] = x + (nn(w["tdT"][...], act) + column(w["pb"][...]))
    xh2, _ = standardize(v["mid"][...])
    v["ren"][0:p] = (xh2 * w["g2"][...] + w["b2"][...]).astype(BF)


def forward_channel(v, p, w):
    ff = w["w1"].shape[1]
    cuts = [slice(j, j + FB) for j in range(0, ff, FB)]
    pre = nn(v["ren"][0:p], w["w1"][:, cuts[0]])
    total = None
    for j, cut in enumerate(cuts):
        ahead = nn(v["ren"][0:p], w["w1"][:, cuts[j + 1]]) if j + 1 < len(cuts) else None
        if j > 0:
            part = nn(v["act"][0:p, cuts[j - 1]], w["w2"][cuts[j - 1], :])
            total = part if total is None else total + part
        act, slope = gelu_parts(pre + w["hb"][:, cut])
        v["act"][0:p, cut] = act
        v["gp"][:, cut] = slope
        pre = ahead
    total = total + nn(v["act"][0:p, cuts[-1]], w["w2"][cuts[-1], :])
    v["out"][...] = (v["mid"][...] + (total + w["ob"][...])).astype(BF)


def back_slot(v, x, og, p, w, tab, second, wide_done):
    v["og"][0:p] = og
    ff = v["pg"].shape[1]
    width = tab.shape[1]

    def through_down(cut):
        return nn(og, w["w2T"][:, cut]) if "w2T" in w else nt(og, w["w2"][cut, :])

    def through_up(cut):
        pre_grad = v["pg"][0:p, cut]
        return nn(pre_grad, w["w1T"][cut, :]) if "w1T" in w else nt(pre_grad, w["w1"][:, cut])

    cuts = [slice(j, j + BB) for j in range(0, ff, BB)]
    act_grad = through_down(cuts[0])
    norm_grad = None
    for j, cut in enumerate(cuts):
        ahead = through_down(cuts[j + 1]) if j + 1 < len(cuts) else None
        if j > 0:
            if j == 1:
                second()
            part = through_up(cuts[j - 1])
            norm_grad = part if norm_grad is None else norm_grad + part
        pre_grad = act_grad * v["gp"][:, cut].astype(F32)
        v["pg"][0:p, cut] = pre_grad.astype(BF)
        sums = rows_sum(pre_grad)
        for k in range(0, BB, 128):
            c, o = divmod(j * BB + k, width)
            tab[HB0 + c : HB0 + c + 1, o : o + 128] += sums[:, k : k + 128]
        act_grad = ahead
    norm_grad = norm_grad + through_up(cuts[-1])
    wide_done()
    xh2, inv2 = standardize(v["mid"][...])
    live = og.astype(F32)
    add_row(tab, OB0, rows_sum(live))
    add_row(tab, SG0, rows_sum(norm_grad * xh2))
    add_row(tab, SS0, rows_sum(norm_grad))
    middle_grad = live + norm_back(w["g2"][...] * norm_grad, xh2, inv2)
    mix = middle_grad.astype(BF)
    v["mix"][...] = mix
    tpg = (nn(w["td"][...], mix) * v["tgp"][...].astype(F32)).astype(BF)
    v["tpg"][...] = tpg
    first_grad = nn(w["tu"][...], tpg)
    xh, inv = standardize(x)
    add_row(tab, FG0, rows_sum(first_grad * xh))
    add_row(tab, FS0, rows_sum(first_grad))
    v["ing"][...] = (middle_grad + norm_back(w["g1"][...] * first_grad, xh, inv)).astype(BF)


def token_slot(normed, tact, mix, tpg, p, tab):
    ones = jnp.ones((8, mix.shape[-1]), BF)
    tab[TB0 : TB0 + 8, :] += nt(ones, tpg)
    tab[PB0 : PB0 + 8, 0:p] += nt(ones, mix)
    tab[TU0 : TU0 + p, :] += nt(normed, tpg)
    tab[TD0 : TD0 + p, :] += nt(mix, tact)


GROUP_TOKEN = ("normed", "tact", "tgp", "mid", "ren")
GROUP_CHANNEL = ("act", "gp", "out")
GROUP_WIDE = ("og", "pg")
GROUP_BACK = ("mix", "tpg", "ing")


def stage_kernel(plan, *refs):
    mode, lo, m, p = plan["mode"], plan["lo"], plan["m"], plan["p"]
    it = iter(refs)
    sc = next(it)
    ins = {name: [next(it) for _ in range(m if alone else 1)] for name, alone in plan["single"].items()}
    sources = {name: next(it) for name in plan["weights"]}
    for _ in range(plan["threaded"]):
        next(it)
    outs = {name: next(it) for name in plan["outs"]}
    send = [next(it) for _ in range(m)] if plan["send"] else None
    v = {name: next(it) for name in plan["buffers"]}
    tab = next(it) if "tab" in outs else None
    zero, blank_out = (next(it), next(it)) if plan["zeros"] else (None, None)
    w = {name: next(it) for name in plan["weights"]}
    for name in plan["turned"]:
        w[name] = next(it)
    in_sem, out_sem, tab_sem, load_sem = next(it), next(it), next(it), next(it)

    if "vec" in w:
        for row, (name, width) in enumerate(plan["rows"].items()):
            w[name] = w["vec"].at[row : row + 1, 0:width]
        w["tu"], w["tdT"] = w["tok"].at[0], w["tok"].at[1]
    mine = sc[1] == plan["flag"]
    live = jnp.where(mine, jnp.clip(sc[0] - lo, 0, m), 0)
    moved = plan["moved"]

    def load(name):
        return pltpu.make_async_copy(sources[name], w[name], load_sem.at[plan["weights"].index(name)])

    def in_copies(i):
        return [
            pltpu.make_async_copy(
                refs[i] if plan["single"][name] else refs[0].at[lo + i], v[name].at[i], in_sem.at[k, i]
            )
            for k, (name, refs) in enumerate(ins.items())
        ]

    def out_copies(names, i):
        return [
            pltpu.make_async_copy(v[name], outs[name].at[lo + i], out_sem.at[moved.index(name)])
            for name in names
            if name in moved
        ]

    def table(inward):
        rows = slice(FG0, TB0) if mode == "both" else slice(0, TROWS)
        a, b = outs["tab"].at[rows], tab.at[rows]
        return pltpu.make_async_copy(a if inward else b, b if inward else a, tab_sem.at[0])

    def send_copy(i):
        return pltpu.make_async_copy(v[plan["send"]], send[i], out_sem.at[len(moved)])

    def switch(i, action):
        for k in range(m):
            pl.when(i == k)(functools.partial(action, k))

    def zero_copy(name, i):
        source = blank_out if name in ZERO_OUT else zero.at[:, 0 : v[name].shape[-1]]
        return pltpu.make_async_copy(source, outs[name].at[lo + i], tab_sem.at[1])

    def start_all(copies):
        for c in copies:
            c.start()

    def wait_all(copies):
        for c in copies:
            c.wait()

    def first_wait(i, names):
        @pl.when(i == 0)
        def _():
            wait_all([load(name) for name in names])

    def free(i, group):
        @pl.when(i > 0)
        def _():
            wait_all(out_copies(group, i - 1))
            if send is not None and plan["send"] in group:
                send_copy(0).wait()

    blank = jnp.logical_and(mine, live < m)
    if plan["zeros"]:
        @pl.when(blank)
        def _():
            zero[...] = jnp.zeros_like(zero)
            blank_out[...] = jnp.zeros_like(blank_out)
            for i in range(m):
                @pl.when(i >= live)
                def _():
                    start_all([zero_copy(n, i) for n in plan["zeros"]])

    small = [n for n in plan["weights"] if n not in LARGE]

    @pl.when(live > 0)
    def _():
        start_all(in_copies(0))
        for name in plan["weights"]:
            if name in small:
                load(name).start()
        if tab is not None:
            table(True).start()
        for name in ("w1", "w2") if mode != "back" else ("w2", "w1"):
            load(name).start()
        for name in ZERO_WIDE:
            if name in v:
                v[name][p:, :] = jnp.zeros((v[name].shape[0] - p, v[name].shape[1]), BF)
        wait_all([load(name) for name in small])
        for name in plan["turned"]:
            source = {"tuT": "tu", "td": "tdT"}[name]
            w[name][...] = jnp.transpose(w[source][...].astype(F32)).astype(BF)
        if tab is not None:
            table(True).wait()

    def slot(i, carry):
        switch(i, lambda k: wait_all(in_copies(k)))
        for k in range(1, m):
            pl.when(jnp.logical_and(i == k - 1, k < live))(functools.partial(lambda k: start_all(in_copies(k)), k))
        x = v["x"][i].astype(F32)
        cot = v["cot"][i] if mode != "forward" else None
        if mode != "back":
            free(i, GROUP_TOKEN)
            forward_token(v, x, p, w)
            start_all(out_copies(GROUP_TOKEN, i))
            first_wait(i, ("w1", "w2"))
            if mode == "both":
                @pl.when(i == 0)
                def _():
                    start_all([load(n) for n in ("w2T", "w1T")])

            free(i, GROUP_CHANNEL)
            forward_channel(v, p, w)
            if mode == "forward":
                switch(i, lambda k: send_copy(k).start())
            start_all(out_copies(GROUP_CHANNEL, i))
        if mode != "forward":
            first_wait(i, ("w2T", "w1T") if mode == "both" else ("w2",))
            free(i, GROUP_WIDE + GROUP_BACK)
            kept = v if mode == "both" else {**v, **{n: v[n].at[i] for n in ("gp", "tgp", "mid", "normed", "tact")}}
            wide_done = lambda: start_all(out_copies(GROUP_WIDE, i))
            second = lambda: first_wait(i, ("w1",)) if mode == "back" else None
            back_slot(kept, x, cot, p, w, tab, second, wide_done)
            if mode == "both":
                switch(i, lambda k: send_copy(k).start())
            start_all(out_copies(GROUP_BACK, i))
            if mode == "back":
                token_slot(kept["normed"][...], kept["tact"][...], v["mix"][...], v["tpg"][...], p, tab)
        return carry

    lax.fori_loop(0, live, slot, 0)

    @pl.when(live > 0)
    def _():
        if tab is not None:
            table(False).start()
            table(False).wait()
        wait_all(out_copies(GROUP_TOKEN + GROUP_CHANNEL + GROUP_WIDE + GROUP_BACK, live - 1))
        if send is not None:
            send_copy(0).wait()

    if plan["zeros"]:
        @pl.when(blank)
        def _():
            for i in range(m):
                @pl.when(i >= live)
                def _():
                    wait_all([zero_copy(n, i) for n in plan["zeros"]])


ROWS = ("g1", "b1", "g2", "b2", "ob", "hb", "tb", "pb")
LARGE = ("w1", "w2", "w1T", "w2T")


def stage(mode, lo, m, sizes, sc, weights, kept, ins):
    slots, p, d, ff, th = sizes
    shapes = shapes_of(*sizes)
    names = {"forward": KEPT_FORWARD, "both": KEPT_BOTH, "back": KEPT_BACK}[mode]
    moved = [n for n in names if n != "tab"]
    zeros = [n for n in names if n in ZERO_WIDE + ZERO_OUT] if lo + m > 1 else []
    keys = ["vec", "tok"] if "vec" in weights else list(ROWS) + ["tu", "tdT"]
    keys += ["w1", "w2"] + (["w1T", "w2T"] if mode == "both" else [])
    turned = {"forward": ["tuT"], "both": ["tuT", "td"], "back": ["td"]}[mode]
    buffers = {
        "forward": ["x"] + moved,
        "both": ["x", "cot"] + moved + ["gp", "tgp", "mid"],
        "back": ["x", "cot", "gp", "tgp", "mid", "normed", "tact", "mix", "tpg"] + moved,
    }[mode]
    threaded = [n for n in names if n in kept]
    single = {n: isinstance(a, list) for n, a in ins.items()}
    shapes.update(x=((slots, p, d), BF), cot=((slots, p, d), BF))

    given = [a for n, arrays in ins.items() for a in (arrays if single[n] else [arrays])]
    args = [sc] + given + [weights[k] for k in keys]
    specs = [SM] + [FREE if single[n] else ANY for n in ins for _ in range(m if single[n] else 1)] + [ANY] * len(keys)
    aliases = {len(args) + k: names.index(n) for k, n in enumerate(threaded)}
    args += [kept[n] for n in threaded]
    specs += [ANY] * len(threaded)
    out_shape = [jax.ShapeDtypeStruct(*shapes[n]) for n in names]
    send = mode != "back"
    if send:
        out_shape += [jax.ShapeDtypeStruct((p, d), BF)] * m
    scratch = [
        pltpu.VMEM(((m,) if n in ins else ()) + shapes[n][0][1:], shapes[n][1]) for n in buffers
    ]
    if "tab" in names:
        scratch.append(pltpu.VMEM(*shapes["tab"]))
    if zeros:
        scratch += [pltpu.VMEM((padded(p), ff), BF), pltpu.VMEM((p, d), BF)]
    scratch += [pltpu.VMEM(weights[k].shape, weights[k].dtype) for k in keys]
    scratch += [pltpu.VMEM((th, p), BF) for n in turned]
    scratch += [
        pltpu.SemaphoreType.DMA((len(ins), m)),
        pltpu.SemaphoreType.DMA((len(moved) + 1,)),
        pltpu.SemaphoreType.DMA((2,)),
        pltpu.SemaphoreType.DMA((len(keys),)),
    ]
    plan = dict(
        mode=mode, lo=lo, m=m, p=p, flag=0 if mode == "both" else 1, weights=keys,
        threaded=len(threaded), outs=list(names), send={"forward": "out", "both": "ing", "back": None}[mode],
        buffers=buffers, moved=moved, zeros=zeros, turned=turned, single=single, rows=dict(zip(ROWS, (d, d, d, d, d, ff, th, p))),
    )
    outs = pl.pallas_call(
        functools.partial(stage_kernel, plan),
        out_shape=out_shape,
        in_specs=specs,
        out_specs=[ANY] * len(out_shape),
        scratch_shapes=scratch,
        input_output_aliases=aliases,
        compiler_params=pltpu.CompilerParams(vmem_limit_bytes=VMEM_LIMIT),
        cost_estimate=TINY,
        name=f"{mode}_{lo}",
    )(*args)
    new = dict(kept)
    new.update(zip(names, outs))
    return new, (list(outs[-m:]) if send else None)


def token_kernel(p, sc, normed_in, tact_in, mix_in, tpg_in, old, tab_out, normed, tact, mix, tpg, tab, sems, tab_sem):
    live = jnp.where(sc[1] == 0, sc[0], 0)
    pairs = ((normed_in, normed), (tact_in, tact), (mix_in, mix), (tpg_in, tpg))

    def copies(i):
        return [pltpu.make_async_copy(a.at[i], b.at[i], sems.at[k, i]) for k, (a, b) in enumerate(pairs)]

    @pl.when(live > 0)
    def _():
        c = pltpu.make_async_copy(tab_out, tab, tab_sem)
        c.start()

        def begin(i, carry):
            for one in copies(i):
                one.start()
            return carry

        lax.fori_loop(0, live, begin, 0)
        c.wait()

        def work(i, carry):
            for one in copies(i):
                one.wait()
            token_slot(normed[i], tact[i], mix[i], tpg[i], p, tab)
            return carry

        lax.fori_loop(0, live, work, 0)
        c = pltpu.make_async_copy(tab, tab_out, tab_sem)
        c.start()
        c.wait()


def token_grads(sizes, sc, kept):
    slots, p = sizes[:2]
    names = ("normed", "tact", "mix", "tpg")
    shapes = shapes_of(*sizes)
    return pl.pallas_call(
        functools.partial(token_kernel, p),
        out_shape=jax.ShapeDtypeStruct(*shapes["tab"]),
        in_specs=[SM] + [ANY] * 5,
        out_specs=ANY,
        scratch_shapes=[pltpu.VMEM(*shapes[n]) for n in names]
        + [pltpu.VMEM(*shapes["tab"]), pltpu.SemaphoreType.DMA((4, slots)), pltpu.SemaphoreType.DMA],
        input_output_aliases={5: 0},
        compiler_params=pltpu.CompilerParams(vmem_limit_bytes=VMEM_LIMIT),
        cost_estimate=TINY,
        name="token_grads",
    )(sc, *[kept[n] for n in names], kept["tab"])


def packed_weights(weights):
    rows = [weights[n] for n in ROWS]
    pair = [weights["tu"], weights["tdT"]]
    ff = max(r.shape[1] for r in rows)

    given = rows + pair

    def kernel(*refs):
        count = len(given)
        vec, tok = refs[count : count + 2]
        held, sems = refs[count + 2 : -1], refs[-1]
        copies = [pltpu.make_async_copy(a, b, sems.at[k]) for k, (a, b) in enumerate(zip(refs[:count], held))]
        for c in copies:
            c.start()
        vec[...] = jnp.zeros_like(vec)
        for c in copies:
            c.wait()
        for k, r in enumerate(held[: len(rows)]):
            vec[k : k + 1, 0 : r.shape[1]] = r[...]
        for k, r in enumerate(held[len(rows) :]):
            tok[k] = r[...]

    return pl.pallas_call(
        kernel,
        out_shape=[jax.ShapeDtypeStruct((len(rows), ff), F32), jax.ShapeDtypeStruct((2,) + pair[0].shape, BF)],
        in_specs=[ANY] * len(given),
        out_specs=[VM, VM],
        scratch_shapes=[pltpu.VMEM(g.shape, g.dtype) for g in given] + [pltpu.SemaphoreType.DMA((len(given),))],
        compiler_params=pltpu.CompilerParams(vmem_limit_bytes=VMEM_LIMIT),
        cost_estimate=TINY,
        name="packed_weights",
    )(*given)


def turned_kernel(sc, w1, w2, w1T, w2T, a, b, at, bt, in_sem, out_sem):
    ff = w1.shape[1]
    wide = 512
    blocks = ff // wide

    def ins(j):
        cut = pl.ds(j * wide, wide)
        return [
            pltpu.make_async_copy(w1.at[:, cut], a.at[:, cut], in_sem.at[0, j]),
            pltpu.make_async_copy(w2.at[cut], b.at[cut], in_sem.at[1, j]),
        ]

    def outs(j):
        cut = pl.ds(j * wide, wide)
        return [
            pltpu.make_async_copy(at.at[cut], w1T.at[cut], out_sem.at[0, j]),
            pltpu.make_async_copy(bt.at[:, cut], w2T.at[:, cut], out_sem.at[1, j]),
        ]

    @pl.when(sc[1] == 0)
    def _():
        for j in range(blocks):
            for c in ins(j):
                c.start()
        for j in range(blocks):
            for c in ins(j):
                c.wait()
            cut = slice(j * wide, (j + 1) * wide)
            at[cut, :] = jnp.transpose(a[:, cut])
            bt[:, cut] = jnp.transpose(b[cut, :])
            for c in outs(j):
                c.start()
        for j in range(blocks):
            for c in outs(j):
                c.wait()


def turned_weights(sc, w1, w2):
    d, ff = w1.shape
    blocks = ff // 512
    return pl.pallas_call(
        turned_kernel,
        out_shape=[jax.ShapeDtypeStruct((ff, d), BF), jax.ShapeDtypeStruct((d, ff), BF)],
        in_specs=[SM, ANY, ANY],
        out_specs=[ANY, ANY],
        scratch_shapes=[
            pltpu.VMEM((d, ff), BF), pltpu.VMEM((ff, d), BF), pltpu.VMEM((ff, d), BF), pltpu.VMEM((d, ff), BF),
            pltpu.SemaphoreType.DMA((2, blocks)), pltpu.SemaphoreType.DMA((2, blocks)),
        ],
        compiler_params=pltpu.CompilerParams(vmem_limit_bytes=VMEM_LIMIT),
        cost_estimate=TINY,
        name="turned_weights",
    )(sc, w1, w2)


def split_halves(core, full, own, other):
    half = full.shape[1] // 2
    left, right = full[:, :half].astype(BF), full[:, half:].astype(BF)

    @pl.when(core == 0)
    def _():
        own[...] = left
        other[...] = right

    @pl.when(core != 0)
    def _():
        own[...] = right
        other[...] = left


def down_grads(core, act, og):
    rows, ff = act.shape
    d = og.shape[1]
    each = ff // RING

    def kernel(c, a, g, own, other):
        full = tn(a[...], g[...])
        for k in range(2):
            split_halves(c[4], full[k * each : (k + 1) * each], own.at[k], other.at[k])

    shape = jax.ShapeDtypeStruct((RING, each, d // 2), BF)
    block = pl.BlockSpec((2, each, d // 2), lambda j: (j, 0, 0))
    return pl.pallas_call(
        kernel,
        grid=(RING // 2,),
        out_shape=[shape, shape],
        in_specs=[
            SM,
            pl.BlockSpec((rows, 2 * each), lambda j: (0, j)),
            pl.BlockSpec((rows, d), lambda j: (0, 0)),
        ],
        out_specs=[block, block],
        compiler_params=pltpu.CompilerParams(vmem_limit_bytes=VMEM_LIMIT),
        cost_estimate=TINY,
        name="down_grads",
    )(core, act, og)


def up_grads(core, ren, pg, tab):
    rows, d = ren.shape
    ff = pg.shape[1]
    each = ff // RING
    half = d // 2
    small = tab.shape[0] // (2 * RING)

    def kernel(c, r, g, t, own, other):
        full = tn(r[...], g[...])
        for k in range(2):
            part = full[:, k * each : (k + 1) * each]
            top = jnp.concatenate([part[:half], t[0, k]], axis=0).astype(BF)
            low = jnp.concatenate([part[half:], t[1, k]], axis=0).astype(BF)

            @pl.when(c[4] == 0)
            def _():
                own[k] = top
                other[k] = low

            @pl.when(c[4] != 0)
            def _():
                own[k] = low
                other[k] = top

    shape = jax.ShapeDtypeStruct((RING, half + small, each), BF)
    block = pl.BlockSpec((2, half + small, each), lambda j: (j, 0, 0))
    return pl.pallas_call(
        kernel,
        grid=(RING // 2,),
        out_shape=[shape, shape],
        in_specs=[
            SM,
            pl.BlockSpec((rows, d), lambda j: (0, 0)),
            pl.BlockSpec((rows, 2 * each), lambda j: (0, j)),
            pl.BlockSpec((2, 2, small, each), lambda j: (0, j, 0, 0)),
        ],
        out_specs=[block, block],
        compiler_params=pltpu.CompilerParams(vmem_limit_bytes=VMEM_LIMIT),
        cost_estimate=TINY,
        name="up_grads",
    )(core, ren, pg, tab.reshape(2, RING, small, each))


def ring_plan(count):
    chips = count // 2
    order = [c for c in range(chips) if c % 2 == 0] + [c for c in range(chips) if c % 2 == 1][::-1]
    place = {c: i for i, c in enumerate(order)}
    forward = [(2 * c, 2 * order[(place[c] + 1) % chips]) for c in range(chips)]
    backward = [(2 * c + 1, 2 * order[(place[c] - 1) % chips] + 1) for c in range(chips)]
    return forward + backward


def ring_sums(parts, count, me):
    chips = count // 2
    ring = ring_plan(count)
    swap = [(i, i ^ 1) for i in range(count)]

    def chunk(pair, k):
        return sum(lax.dynamic_index_in_dim(a, k % chips, 0, keepdims=False) for a in pair)

    held = [(own, lax.ppermute(other, "dp", swap)) for own, other in parts]
    moving = [chunk(a, me + chips - 1) for a in held]
    for step in range(chips - 1):
        arrived = [lax.ppermute(c, "dp", ring) for c in moving]
        moving = [r + chunk(a, me + 2 * chips - 2 - step) for r, a in zip(arrived, held)]
    mine, theirs = [[c] for c in moving], [[lax.ppermute(c, "dp", swap)] for c in moving]
    for step in range(chips - 1):
        if step > 0:
            for i, c in enumerate(moving):
                moving[i], theirs[i][-2 if step > 1 else -1] = lax.optimization_barrier(
                    (c, theirs[i][-2 if step > 1 else -1])
                )
        moving = [lax.ppermute(c, "dp", ring) for c in moving]
        for i, c in enumerate(moving):
            mine[i].append(c)
            theirs[i].append(lax.ppermute(c, "dp", swap))
    return mine, theirs


def finish_kernel(p, first, last, threaded, *refs):
    it = iter(refs)
    where = next(it)
    steps = range(first, last)
    chunks = [[{s: next(it) for s in steps} for _ in range(2)] for _ in range(2)]
    for _ in range(threaded):
        next(it)
    down, up, tab_out = next(it), next(it), next(it)
    final = last == RING
    if final:
        fg, fs, tu, tb, td, pb, sg, ss, hb, ob = [next(it) for _ in range(10)]
    taken = [next(it), next(it)]
    given = [next(it), next(it)]
    tab = next(it)
    in_sem, out_sem, tab_sem = next(it), next(it), next(it)
    each = down.shape[1] // RING
    half = down.shape[2] // 2
    small = taken[1].shape[1] - half
    jobs = [(kind, side, s) for s in steps for side in range(2) for kind in range(2)]
    depth = taken[0].shape[0]

    def place(side, s):
        at = where[2 + side] + 2 * RING - s
        return lax.rem(at, RING), (where[4] if side == 0 else 1 - where[4])

    def fetch(n):
        kind, side, s = jobs[n]
        slot = n // 2 % depth
        return pltpu.make_async_copy(chunks[kind][side][s], taken[kind].at[slot], in_sem.at[kind, slot])

    def store(n):
        kind, side, s = jobs[n]
        k, h = place(side, s)
        slot = n // 2 % depth
        by_ff = pl.ds(pl.multiple_of(k * each, each), each)
        by_half = pl.ds(pl.multiple_of(h * half, half), half)
        target = down.at[0, by_ff, by_half] if kind == 0 else up.at[0, by_half, by_ff]
        return pltpu.make_async_copy(given[kind].at[slot], target, out_sem.at[kind, slot])

    def old_table():
        return pltpu.make_async_copy(tab_out, tab, tab_sem)

    lag = 2 * depth
    if first > 0:
        old_table().start()
    for n in range(min(lag, len(jobs))):
        fetch(n).start()
    if first > 0:
        old_table().wait()
    for n, (kind, side, s) in enumerate(jobs):
        fetch(n).wait()
        if n >= lag:
            store(n - lag).wait()
        slot = n // 2 % depth
        given[kind][slot] = taken[kind][slot, 0:half].astype(F32)
        store(n).start()
        if kind == 1:
            k, h = place(side, s)
            tab[pl.ds(pl.multiple_of((h * RING + k) * small, small), small), :] = taken[1][slot, half:].astype(F32)
        if n + lag < len(jobs):
            fetch(n + lag).start()
    keep = pltpu.make_async_copy(tab, tab_out, tab_sem)
    keep.start()

    def vector(ref, row):
        width = tab.shape[1]
        length = ref.shape[1]
        for i in range(-(-length // width)):
            size = min(width, length - i * width)
            ref[:, i * width : i * width + size] = tab[row + i : row + i + 1, 0:size]

    if final:
        tu[:, 0, :] = tab[TU0 : TU0 + p, :]
        td[:, 0, :] = tab[TD0 : TD0 + p, :]
        for ref, row in ((fg, FG0), (fs, FS0), (tb, TB0), (pb, PB0), (sg, SG0), (ss, SS0), (hb, HB0), (ob, OB0)):
            vector(ref, row)
    for n in range(max(0, len(jobs) - lag), len(jobs)):
        store(n).wait()
    keep.wait()


def finish(where, mine, theirs, sizes):
    slots, p, d, ff, th = sizes
    half, each = d // 2, ff // RING
    rows = mine[1][0].shape[0]
    big = [jax.ShapeDtypeStruct(s, F32) for s in ((1, ff, d), (1, d, ff), (TROWS, th))]
    few = [
        jax.ShapeDtypeStruct(s, F32)
        for s in ((1, d), (1, d), (p, 1, th), (1, th), (p, 1, th), (1, p), (1, d), (1, d), (1, ff), (1, d))
    ]
    depth = 4
    scratch = [pltpu.VMEM((depth, half, each), BF), pltpu.VMEM((depth, rows, each), BF)]
    scratch += [pltpu.VMEM((depth, half, each), F32), pltpu.VMEM((depth, half, each), F32)]
    scratch += [
        pltpu.VMEM((TROWS, th), F32), pltpu.SemaphoreType.DMA((2, depth)), pltpu.SemaphoreType.DMA((2, depth)),
        pltpu.SemaphoreType.DMA,
    ]
    results = []
    for first, last in FINISH:
        args = [side[kind][s] for kind in range(2) for side in (mine, theirs) for s in range(first, last)]
        aliases = {1 + len(args) + i: i for i in range(len(results))}
        final = last == RING
        out = pl.pallas_call(
            functools.partial(finish_kernel, p, first, last, len(results)),
            out_shape=big + (few if final else []),
            in_specs=[SM] + [FREE] * len(args) + [ANY] * len(results),
            out_specs=[ANY] * 3 + ([VM] * len(few) if final else []),
            scratch_shapes=scratch,
            input_output_aliases=aliases,
            compiler_params=pltpu.CompilerParams(vmem_limit_bytes=VMEM_LIMIT),
            cost_estimate=pl.CostEstimate(
                flops=1 << 10, bytes_accessed=(last - first) * (4 << 20), transcendentals=0
            ),
            name=f"finish_{first}",
        )(where, *args, *results)
        results = list(out[:3])
    fg, fs, tu, tb, td, pb, sg, ss, hb, ob = out[3:]
    down, up = results[:2]
    return down, up, fg, fs, tu.transpose(1, 0, 2), tb, td.transpose(1, 2, 0), pb, sg, ss, hb, ob


def body(images, cotangent, image_counts, first_gain, first_shift, token_up, token_bias, token_down, patch_bias,
         second_gain, second_shift, channel_up, hidden_bias, channel_down, output_bias):
    slots, p, d = images.shape
    ff, th = channel_up.shape[2], token_up.shape[2]
    sizes = (slots, p, d, ff, th)
    count = lax.axis_size("dp")
    leading = lax.axis_index("section") == 0
    index = lax.axis_index("dp")
    core, chip = index % 2, index // 2
    spot = jnp.where(chip % 2 == 0, chip // 2, count // 2 - 1 - chip // 2)
    turned_spot = count // 2 - 1 - spot
    spots = (jnp.where(core == 0, spot, turned_spot), jnp.where(core == 0, turned_spot, spot))
    sc = jnp.stack([image_counts[0], leading.astype(jnp.int32), *spots, core.astype(jnp.int32)])
    weights = dict(
        g1=first_gain, b1=first_shift, tu=token_up[0], tb=token_bias, tdT=token_down[0].T, pb=patch_bias,
        g2=second_gain, b2=second_shift, w1=channel_up[0], hb=hidden_bias, w2=channel_down[0], ob=output_bias,
    )
    cuts = [(0, 1)] + [(lo, min(2, slots - 1 - lo)) for lo in range(1, slots - 1, 2)] + [(slots - 1, 1)]

    kept, sent, returned = {}, [], []

    def forward(number):
        nonlocal kept
        lo, m = cuts[number]
        kept, out = stage("forward", lo, m, sizes, sc, weights, kept, {"x": images})
        sent.append([lax.ppermute(o, "section", [(0, 1)]) for o in out])

    def both(number):
        nonlocal kept
        lo, m = cuts[number]
        ins = {"x": sent[number], "cot": cotangent}
        kept, grad = stage("both", lo, m, sizes, sc, weights, kept, ins)
        returned.append([lax.ppermute(g, "section", [(1, 0)]) for g in grad])

    def back(numbers):
        nonlocal kept
        lo, m = cuts[numbers[0]][0], sum(cuts[n][1] for n in numbers)
        ins = {"x": images, "cot": [g for n in numbers for g in returned[n]]}
        ins.update({n: kept[n] for n in ("gp", "tgp", "mid", "normed", "tact")})
        kept, _ = stage("back", lo, m, sizes, sc, weights, kept, ins)

    last = len(cuts) - 1
    forward(0)
    forward(1)
    pb, kept["act"] = lax.optimization_barrier((weights["pb"], kept["act"]))
    weights["vec"], weights["tok"] = packed_weights(dict(weights, pb=pb))
    w1, w2, kept["act"] = lax.optimization_barrier((weights["w1"], weights["w2"], kept["act"]))
    weights["w1T"], weights["w2T"] = turned_weights(sc, w1, w2)
    kept["tab"] = jnp.zeros((TROWS, th), F32)
    assert last >= 3
    for number in range(last + 1):
        if number >= 3:
            back([0, 1] if number == 3 else [number - 2])
        both(number)
        if number + 2 <= last:
            forward(number + 2)
    back([last - 1])
    back([last])

    flat = {n: kept[n].reshape(-1, kept[n].shape[-1]) for n in ("act", "ren", "og", "pg")}
    down = down_grads(sc, flat["act"], flat["og"])
    tab = token_grads(sizes, sc, kept)
    up = up_grads(sc, flat["ren"], flat["pg"], tab)
    if count == 2 * RING:
        mine, theirs = ring_sums([down, up], count, spots[0])
        where = sc
    else:
        whole = [jnp.where(core == 0, jnp.stack(pair), jnp.stack(pair[::-1])) for pair in (down, up)]
        whole = [w.astype(BF) for w in lax.psum([w.astype(F32) for w in whole], "dp")]
        mine = [[w[0, -s % RING] for s in range(RING)] for w in whole]
        theirs = [[w[1, -s % RING] for s in range(RING)] for w in whole]
        where = jnp.zeros_like(sc)
    grads = finish(where, mine, theirs, sizes)
    down_sum, up_sum, fg, fs, tu, tb, td, pb, sg, ss, hb, ob = grads
    return (kept["out"][None], kept["ing"][None], fg, fs, tu, tb, td, pb, sg, ss, up_sum, hb, down_sum, ob)


def solution(mesh):
    row = P("section", None)
    mat = P("section", None, None)
    in_specs = (
        P("dp", None, None), P("dp", None, None), P("dp"), row, row, mat, row, mat, row, row, row, mat, row, mat, row,
    )
    stream = P("section", "dp", None, None)
    out_specs = (stream, stream, row, row, mat, row, mat, row, row, row, mat, row, mat, row)
    return jax.shard_map(body, mesh=mesh, in_specs=in_specs, out_specs=out_specs, check_vma=False)
```

```python
import functools
import math

import jax
import jax.numpy as jnp
from jax import lax
from jax.experimental import pallas as pl
from jax.experimental.pallas import tpu as pltpu
from jax.sharding import PartitionSpec as P

EPS = 1e-06
BF, F32 = jnp.bfloat16, jnp.float32
HALF_ROOT = math.sqrt(0.5)
PEAK = 1.0 / math.sqrt(2.0 * math.pi)
FB, BB = 1024, 512
VMEM_LIMIT = 63 << 20
RING = 8
FINISH = ((0, 8),)

ANY = pl.BlockSpec(memory_space=pltpu.HBM)
FREE = pl.BlockSpec(memory_space=pl.ANY)
VM = pl.BlockSpec(memory_space=pltpu.VMEM)
SM = pl.BlockSpec(memory_space=pltpu.SMEM)
TINY = pl.CostEstimate(flops=1 << 10, bytes_accessed=1 << 10, transcendentals=0)

TU0, TD0, FG0, FS0, SG0, SS0, OB0, HB0, TB0, PB0, TROWS = 0, 200, 400, 402, 404, 406, 408, 416, 424, 432, 512

KEPT_FORWARD = ("act", "ren", "normed", "tact", "out", "gp", "tgp", "mid")
KEPT_BOTH = ("act", "ren", "normed", "tact", "out", "og", "pg", "mix", "tpg", "ing", "tab")
KEPT_BACK = ("og", "pg", "ing", "tab")
ZERO_WIDE = ("act", "ren", "og", "pg")
ZERO_OUT = ("out", "ing")


def nn(a, b):
    return jnp.dot(a, b, preferred_element_type=F32)


def nt(a, b):
    return lax.dot_general(a, b, (((1,), (1,)), ((), ())), preferred_element_type=F32)


def tn(a, b):
    return lax.dot_general(a, b, (((0,), (0,)), ((), ())), preferred_element_type=F32)


def padded(rows):
    return -(-rows // 16) * 16


def gelu_parts(z):
    u = z * HALF_ROOT
    phi = 0.5 + 0.5 * lax.erf(u)
    slope = phi + (z * PEAK) * jnp.exp(-(u * u))
    return (z * phi).astype(BF), slope.astype(BF)


def standardize(v):
    center = v - jnp.mean(v, axis=-1, keepdims=True)
    spread = jnp.mean(center * center, axis=-1, keepdims=True)
    inverse = lax.rsqrt(spread + EPS)
    return center * inverse, inverse


def norm_back(y, xhat, inverse):
    return (
        y - jnp.mean(y, axis=-1, keepdims=True) - xhat * jnp.mean(y * xhat, axis=-1, keepdims=True)
    ) * inverse


def rows_sum(v):
    return jnp.sum(v, axis=0, keepdims=True)


def add_row(tab, row, vec):
    width = tab.shape[1]
    for i in range(vec.shape[1] // width):
        tab[row + i : row + i + 1, :] += vec[:, i * width : (i + 1) * width]


def column(row):
    return jnp.transpose(jnp.broadcast_to(row, (8, row.shape[1])))[:, 0:1]


def shapes_of(slots, p, d, ff, th):
    q = padded(p)
    return dict(
        act=((slots, q, ff), BF),
        ren=((slots, q, d), BF),
        og=((slots, q, d), BF),
        pg=((slots, q, ff), BF),
        gp=((slots, p, ff), BF),
        normed=((slots, p, d), BF),
        tact=((slots, th, d), BF),
        tgp=((slots, th, d), BF),
        tpg=((slots, th, d), BF),
        mix=((slots, p, d), BF),
        mid=((slots, p, d), F32),
        out=((slots, p, d), BF),
        ing=((slots, p, d), BF),
        tab=((TROWS, th), F32),
    )


def forward_token(v, x, p, w):
    xh, _ = standardize(x)
    normed = (xh * w["g1"][...] + w["b1"][...]).astype(BF)
    v["normed"][...] = normed
    act, slope = gelu_parts(nn(w["tuT"][...], normed) + column(w["tb"][...]))
    v["tact"][...] = act
    v["tgp"][...] = slope
    v["mid"][...] = x + (nn(w["tdT"][...], act) + column(w["pb"][...]))
    xh2, _ = standardize(v["mid"][...])
    v["ren"][0:p] = (xh2 * w["g2"][...] + w["b2"][...]).astype(BF)


def forward_channel(v, p, w):
    ff = w["w1"].shape[1]
    cuts = [slice(j, j + FB) for j in range(0, ff, FB)]
    pre = nn(v["ren"][0:p], w["w1"][:, cuts[0]])
    total = None
    for j, cut in enumerate(cuts):
        ahead = nn(v["ren"][0:p], w["w1"][:, cuts[j + 1]]) if j + 1 < len(cuts) else None
        if j > 0:
            part = nn(v["act"][0:p, cuts[j - 1]], w["w2"][cuts[j - 1], :])
            total = part if total is None else total + part
        act, slope = gelu_parts(pre + w["hb"][:, cut])
        v["act"][0:p, cut] = act
        v["gp"][:, cut] = slope
        pre = ahead
    total = total + nn(v["act"][0:p, cuts[-1]], w["w2"][cuts[-1], :])
    v["out"][...] = (v["mid"][...] + (total + w["ob"][...])).astype(BF)


def back_slot(v, x, og, p, w, tab, second, wide_done):
    v["og"][0:p] = og
    ff = v["pg"].shape[1]
    width = tab.shape[1]

    def through_down(cut):
        return nn(og, w["w2T"][:, cut]) if "w2T" in w else nt(og, w["w2"][cut, :])

    def through_up(cut):
        pre_grad = v["pg"][0:p, cut]
        return nn(pre_grad, w["w1T"][cut, :]) if "w1T" in w else nt(pre_grad, w["w1"][:, cut])

    cuts = [slice(j, j + BB) for j in range(0, ff, BB)]
    act_grad = through_down(cuts[0])
    norm_grad = None
    for j, cut in enumerate(cuts):
        ahead = through_down(cuts[j + 1]) if j + 1 < len(cuts) else None
        if j > 0:
            if j == 1:
                second()
            part = through_up(cuts[j - 1])
            norm_grad = part if norm_grad is None else norm_grad + part
        pre_grad = act_grad * v["gp"][:, cut].astype(F32)
        v["pg"][0:p, cut] = pre_grad.astype(BF)
        sums = rows_sum(pre_grad)
        for k in range(0, BB, 128):
            c, o = divmod(j * BB + k, width)
            tab[HB0 + c : HB0 + c + 1, o : o + 128] += sums[:, k : k + 128]
        act_grad = ahead
    norm_grad = norm_grad + through_up(cuts[-1])
    wide_done()
    xh2, inv2 = standardize(v["mid"][...])
    live = og.astype(F32)
    add_row(tab, OB0, rows_sum(live))
    add_row(tab, SG0, rows_sum(norm_grad * xh2))
    add_row(tab, SS0, rows_sum(norm_grad))
    middle_grad = live + norm_back(w["g2"][...] * norm_grad, xh2, inv2)
    mix = middle_grad.astype(BF)
    v["mix"][...] = mix
    tpg = (nn(w["td"][...], mix) * v["tgp"][...].astype(F32)).astype(BF)
    v["tpg"][...] = tpg
    first_grad = nn(w["tu"][...], tpg)
    xh, inv = standardize(x)
    add_row(tab, FG0, rows_sum(first_grad * xh))
    add_row(tab, FS0, rows_sum(first_grad))
    v["ing"][...] = (middle_grad + norm_back(w["g1"][...] * first_grad, xh, inv)).astype(BF)


def token_slot(normed, tact, mix, tpg, p, tab):
    ones = jnp.ones((8, mix.shape[-1]), BF)
    tab[TB0 : TB0 + 8, :] += nt(ones, tpg)
    tab[PB0 : PB0 + 8, 0:p] += nt(ones, mix)
    tab[TU0 : TU0 + p, :] += nt(normed, tpg)
    tab[TD0 : TD0 + p, :] += nt(mix, tact)


GROUP_TOKEN = ("normed", "tact", "tgp", "mid", "ren")
GROUP_CHANNEL = ("act", "gp", "out")
GROUP_WIDE = ("og", "pg")
GROUP_BACK = ("mix", "tpg", "ing")


def stage_kernel(plan, *refs):
    mode, lo, m, p = plan["mode"], plan["lo"], plan["m"], plan["p"]
    it = iter(refs)
    sc = next(it)
    ins = {name: [next(it) for _ in range(m if alone else 1)] for name, alone in plan["single"].items()}
    sources = {name: next(it) for name in plan["weights"]}
    for _ in range(plan["threaded"]):
        next(it)
    outs = {name: next(it) for name in plan["outs"]}
    send = [next(it) for _ in range(m)] if plan["send"] else None
    v = {name: next(it) for name in plan["buffers"]}
    tab = next(it) if "tab" in outs else None
    zero, blank_out = (next(it), next(it)) if plan["zeros"] else (None, None)
    w = {name: next(it) for name in plan["weights"]}
    for name in plan["turned"]:
        w[name] = next(it)
    in_sem, out_sem, tab_sem, load_sem = next(it), next(it), next(it), next(it)

    if "vec" in w:
        for row, (name, width) in enumerate(plan["rows"].items()):
            w[name] = w["vec"].at[row : row + 1, 0:width]
        w["tu"], w["tdT"] = w["tok"].at[0], w["tok"].at[1]
    mine = sc[1] == plan["flag"]
    live = jnp.where(mine, jnp.clip(sc[0] - lo, 0, m), 0)
    moved = plan["moved"]

    def load(name):
        return pltpu.make_async_copy(sources[name], w[name], load_sem.at[plan["weights"].index(name)])

    def in_copies(i):
        return [
            pltpu.make_async_copy(
                refs[i] if plan["single"][name] else refs[0].at[lo + i], v[name].at[i], in_sem.at[k, i]
            )
            for k, (name, refs) in enumerate(ins.items())
        ]

    def out_copies(names, i):
        return [
            pltpu.make_async_copy(v[name], outs[name].at[lo + i], out_sem.at[moved.index(name)])
            for name in names
            if name in moved
        ]

    def table(inward):
        rows = slice(FG0, TB0) if mode == "both" else slice(0, TROWS)
        a, b = outs["tab"].at[rows], tab.at[rows]
        return pltpu.make_async_copy(a if inward else b, b if inward else a, tab_sem.at[0])

    def send_copy(i):
        return pltpu.make_async_copy(v[plan["send"]], send[i], out_sem.at[len(moved)])

    def switch(i, action):
        for k in range(m):
            pl.when(i == k)(functools.partial(action, k))

    def zero_copy(name, i):
        source = blank_out if name in ZERO_OUT else zero.at[:, 0 : v[name].shape[-1]]
        return pltpu.make_async_copy(source, outs[name].at[lo + i], tab_sem.at[1])

    def start_all(copies):
        for c in copies:
            c.start()

    def wait_all(copies):
        for c in copies:
            c.wait()

    def first_wait(i, names):
        @pl.when(i == 0)
        def _():
            wait_all([load(name) for name in names])

    def free(i, group):
        @pl.when(i > 0)
        def _():
            wait_all(out_copies(group, i - 1))
            if send is not None and plan["send"] in group:
                send_copy(0).wait()

    blank = jnp.logical_and(mine, live < m)
    if plan["zeros"]:
        @pl.when(blank)
        def _():
            zero[...] = jnp.zeros_like(zero)
            blank_out[...] = jnp.zeros_like(blank_out)
            for i in range(m):
                @pl.when(i >= live)
                def _():
                    start_all([zero_copy(n, i) for n in plan["zeros"]])

    small = [n for n in plan["weights"] if n not in LARGE]

    @pl.when(live > 0)
    def _():
        start_all(in_copies(0))
        for name in plan["weights"]:
            if name in small:
                load(name).start()
        if tab is not None:
            table(True).start()
        for name in ("w1", "w2") if mode != "back" else ("w2", "w1"):
            load(name).start()
        for name in ZERO_WIDE:
            if name in v:
                v[name][p:, :] = jnp.zeros((v[name].shape[0] - p, v[name].shape[1]), BF)
        wait_all([load(name) for name in small])
        for name in plan["turned"]:
            source = {"tuT": "tu", "td": "tdT"}[name]
            w[name][...] = jnp.transpose(w[source][...].astype(F32)).astype(BF)
        if tab is not None:
            table(True).wait()

    def slot(i, carry):
        switch(i, lambda k: wait_all(in_copies(k)))
        for k in range(1, m):
            pl.when(jnp.logical_and(i == k - 1, k < live))(functools.partial(lambda k: start_all(in_copies(k)), k))
        x = v["x"][i].astype(F32)
        cot = v["cot"][i] if mode != "forward" else None
        if mode != "back":
            free(i, GROUP_TOKEN)
            forward_token(v, x, p, w)
            start_all(out_copies(GROUP_TOKEN, i))
            first_wait(i, ("w1", "w2"))
            if mode == "both":
                @pl.when(i == 0)
                def _():
                    start_all([load(n) for n in ("w2T", "w1T")])

            free(i, GROUP_CHANNEL)
            forward_channel(v, p, w)
            if mode == "forward":
                switch(i, lambda k: send_copy(k).start())
            start_all(out_copies(GROUP_CHANNEL, i))
        if mode != "forward":
            first_wait(i, ("w2T", "w1T") if mode == "both" else ("w2",))
            free(i, GROUP_WIDE + GROUP_BACK)
            kept = v if mode == "both" else {**v, **{n: v[n].at[i] for n in ("gp", "tgp", "mid", "normed", "tact")}}
            wide_done = lambda: start_all(out_copies(GROUP_WIDE, i))
            second = lambda: first_wait(i, ("w1",)) if mode == "back" else None
            back_slot(kept, x, cot, p, w, tab, second, wide_done)
            if mode == "both":
                switch(i, lambda k: send_copy(k).start())
            start_all(out_copies(GROUP_BACK, i))
            if mode == "back":
                token_slot(kept["normed"][...], kept["tact"][...], v["mix"][...], v["tpg"][...], p, tab)
        return carry

    lax.fori_loop(0, live, slot, 0)

    @pl.when(live > 0)
    def _():
        if tab is not None:
            table(False).start()
            table(False).wait()
        wait_all(out_copies(GROUP_TOKEN + GROUP_CHANNEL + GROUP_WIDE + GROUP_BACK, live - 1))
        if send is not None:
            send_copy(0).wait()

    if plan["zeros"]:
        @pl.when(blank)
        def _():
            for i in range(m):
                @pl.when(i >= live)
                def _():
                    wait_all([zero_copy(n, i) for n in plan["zeros"]])


ROWS = ("g1", "b1", "g2", "b2", "ob", "hb", "tb", "pb")
LARGE = ("w1", "w2", "w1T", "w2T")


def stage(mode, lo, m, sizes, sc, weights, kept, ins):
    slots, p, d, ff, th = sizes
    shapes = shapes_of(*sizes)
    names = {"forward": KEPT_FORWARD, "both": KEPT_BOTH, "back": KEPT_BACK}[mode]
    moved = [n for n in names if n != "tab"]
    zeros = [n for n in names if n in ZERO_WIDE + ZERO_OUT] if lo + m > 1 else []
    keys = ["vec", "tok"] if "vec" in weights else list(ROWS) + ["tu", "tdT"]
    keys += ["w1", "w2"] + (["w1T", "w2T"] if mode == "both" else [])
    turned = {"forward": ["tuT"], "both": ["tuT", "td"], "back": ["td"]}[mode]
    buffers = {
        "forward": ["x"] + moved,
        "both": ["x", "cot"] + moved + ["gp", "tgp", "mid"],
        "back": ["x", "cot", "gp", "tgp", "mid", "normed", "tact", "mix", "tpg"] + moved,
    }[mode]
    threaded = [n for n in names if n in kept]
    single = {n: isinstance(a, list) for n, a in ins.items()}
    shapes.update(x=((slots, p, d), BF), cot=((slots, p, d), BF))

    given = [a for n, arrays in ins.items() for a in (arrays if single[n] else [arrays])]
    args = [sc] + given + [weights[k] for k in keys]
    specs = [SM] + [FREE if single[n] else ANY for n in ins for _ in range(m if single[n] else 1)] + [ANY] * len(keys)
    aliases = {len(args) + k: names.index(n) for k, n in enumerate(threaded)}
    args += [kept[n] for n in threaded]
    specs += [ANY] * len(threaded)
    out_shape = [jax.ShapeDtypeStruct(*shapes[n]) for n in names]
    send = mode != "back"
    if send:
        out_shape += [jax.ShapeDtypeStruct((p, d), BF)] * m
    scratch = [
        pltpu.VMEM(((m,) if n in ins else ()) + shapes[n][0][1:], shapes[n][1]) for n in buffers
    ]
    if "tab" in names:
        scratch.append(pltpu.VMEM(*shapes["tab"]))
    if zeros:
        scratch += [pltpu.VMEM((padded(p), ff), BF), pltpu.VMEM((p, d), BF)]
    scratch += [pltpu.VMEM(weights[k].shape, weights[k].dtype) for k in keys]
    scratch += [pltpu.VMEM((th, p), BF) for n in turned]
    scratch += [
        pltpu.SemaphoreType.DMA((len(ins), m)),
        pltpu.SemaphoreType.DMA((len(moved) + 1,)),
        pltpu.SemaphoreType.DMA((2,)),
        pltpu.SemaphoreType.DMA((len(keys),)),
    ]
    plan = dict(
        mode=mode, lo=lo, m=m, p=p, flag=0 if mode == "both" else 1, weights=keys,
        threaded=len(threaded), outs=list(names), send={"forward": "out", "both": "ing", "back": None}[mode],
        buffers=buffers, moved=moved, zeros=zeros, turned=turned, single=single, rows=dict(zip(ROWS, (d, d, d, d, d, ff, th, p))),
    )
    outs = pl.pallas_call(
        functools.partial(stage_kernel, plan),
        out_shape=out_shape,
        in_specs=specs,
        out_specs=[ANY] * len(out_shape),
        scratch_shapes=scratch,
        input_output_aliases=aliases,
        compiler_params=pltpu.CompilerParams(vmem_limit_bytes=VMEM_LIMIT),
        cost_estimate=TINY,
        name=f"{mode}_{lo}",
    )(*args)
    new = dict(kept)
    new.update(zip(names, outs))
    return new, (list(outs[-m:]) if send else None)


def token_kernel(p, sc, normed_in, tact_in, mix_in, tpg_in, old, tab_out, normed, tact, mix, tpg, tab, sems, tab_sem):
    live = jnp.where(sc[1] == 0, sc[0], 0)
    pairs = ((normed_in, normed), (tact_in, tact), (mix_in, mix), (tpg_in, tpg))

    def copies(i):
        return [pltpu.make_async_copy(a.at[i], b.at[i], sems.at[k, i]) for k, (a, b) in enumerate(pairs)]

    @pl.when(live > 0)
    def _():
        c = pltpu.make_async_copy(tab_out, tab, tab_sem)
        c.start()

        def begin(i, carry):
            for one in copies(i):
                one.start()
            return carry

        lax.fori_loop(0, live, begin, 0)
        c.wait()

        def work(i, carry):
            for one in copies(i):
                one.wait()
            token_slot(normed[i], tact[i], mix[i], tpg[i], p, tab)
            return carry

        lax.fori_loop(0, live, work, 0)
        c = pltpu.make_async_copy(tab, tab_out, tab_sem)
        c.start()
        c.wait()


def token_grads(sizes, sc, kept):
    slots, p = sizes[:2]
    names = ("normed", "tact", "mix", "tpg")
    shapes = shapes_of(*sizes)
    return pl.pallas_call(
        functools.partial(token_kernel, p),
        out_shape=jax.ShapeDtypeStruct(*shapes["tab"]),
        in_specs=[SM] + [ANY] * 5,
        out_specs=ANY,
        scratch_shapes=[pltpu.VMEM(*shapes[n]) for n in names]
        + [pltpu.VMEM(*shapes["tab"]), pltpu.SemaphoreType.DMA((4, slots)), pltpu.SemaphoreType.DMA],
        input_output_aliases={5: 0},
        compiler_params=pltpu.CompilerParams(vmem_limit_bytes=VMEM_LIMIT),
        cost_estimate=TINY,
        name="token_grads",
    )(sc, *[kept[n] for n in names], kept["tab"])


def packed_weights(weights):
    rows = [weights[n] for n in ROWS]
    pair = [weights["tu"], weights["tdT"]]
    ff = max(r.shape[1] for r in rows)

    given = rows + pair

    def kernel(*refs):
        count = len(given)
        vec, tok = refs[count : count + 2]
        held, sems = refs[count + 2 : -1], refs[-1]
        copies = [pltpu.make_async_copy(a, b, sems.at[k]) for k, (a, b) in enumerate(zip(refs[:count], held))]
        for c in copies:
            c.start()
        vec[...] = jnp.zeros_like(vec)
        for c in copies:
            c.wait()
        for k, r in enumerate(held[: len(rows)]):
            vec[k : k + 1, 0 : r.shape[1]] = r[...]
        for k, r in enumerate(held[len(rows) :]):
            tok[k] = r[...]

    return pl.pallas_call(
        kernel,
        out_shape=[jax.ShapeDtypeStruct((len(rows), ff), F32), jax.ShapeDtypeStruct((2,) + pair[0].shape, BF)],
        in_specs=[ANY] * len(given),
        out_specs=[VM, VM],
        scratch_shapes=[pltpu.VMEM(g.shape, g.dtype) for g in given] + [pltpu.SemaphoreType.DMA((len(given),))],
        compiler_params=pltpu.CompilerParams(vmem_limit_bytes=VMEM_LIMIT),
        cost_estimate=TINY,
        name="packed_weights",
    )(*given)


def turned_kernel(sc, w1, w2, w1T, w2T, a, b, at, bt, in_sem, out_sem):
    ff = w1.shape[1]
    wide = 512
    blocks = ff // wide

    def ins(j):
        cut = pl.ds(j * wide, wide)
        return [
            pltpu.make_async_copy(w1.at[:, cut], a.at[:, cut], in_sem.at[0, j]),
            pltpu.make_async_copy(w2.at[cut], b.at[cut], in_sem.at[1, j]),
        ]

    def outs(j):
        cut = pl.ds(j * wide, wide)
        return [
            pltpu.make_async_copy(at.at[cut], w1T.at[cut], out_sem.at[0, j]),
            pltpu.make_async_copy(bt.at[:, cut], w2T.at[:, cut], out_sem.at[1, j]),
        ]

    @pl.when(sc[1] == 0)
    def _():
        for j in range(blocks):
            for c in ins(j):
                c.start()
        for j in range(blocks):
            for c in ins(j):
                c.wait()
            cut = slice(j * wide, (j + 1) * wide)
            at[cut, :] = jnp.transpose(a[:, cut])
            bt[:, cut] = jnp.transpose(b[cut, :])
            for c in outs(j):
                c.start()
        for j in range(blocks):
            for c in outs(j):
                c.wait()


def turned_weights(sc, w1, w2):
    d, ff = w1.shape
    blocks = ff // 512
    return pl.pallas_call(
        turned_kernel,
        out_shape=[jax.ShapeDtypeStruct((ff, d), BF), jax.ShapeDtypeStruct((d, ff), BF)],
        in_specs=[SM, ANY, ANY],
        out_specs=[ANY, ANY],
        scratch_shapes=[
            pltpu.VMEM((d, ff), BF), pltpu.VMEM((ff, d), BF), pltpu.VMEM((ff, d), BF), pltpu.VMEM((d, ff), BF),
            pltpu.SemaphoreType.DMA((2, blocks)), pltpu.SemaphoreType.DMA((2, blocks)),
        ],
        compiler_params=pltpu.CompilerParams(vmem_limit_bytes=VMEM_LIMIT),
        cost_estimate=TINY,
        name="turned_weights",
    )(sc, w1, w2)


def split_halves(core, full, own, other):
    half = full.shape[1] // 2
    left, right = full[:, :half].astype(BF), full[:, half:].astype(BF)

    @pl.when(core == 0)
    def _():
        own[...] = left
        other[...] = right

    @pl.when(core != 0)
    def _():
        own[...] = right
        other[...] = left


def down_grads(core, act, og):
    rows, ff = act.shape
    d = og.shape[1]
    each = ff // RING

    def kernel(c, a, g, own, other):
        full = tn(a[...], g[...])
        for k in range(2):
            split_halves(c[4], full[k * each : (k + 1) * each], own.at[k], other.at[k])

    shape = jax.ShapeDtypeStruct((RING, each, d // 2), BF)
    block = pl.BlockSpec((2, each, d // 2), lambda j: (j, 0, 0))
    return pl.pallas_call(
        kernel,
        grid=(RING // 2,),
        out_shape=[shape, shape],
        in_specs=[
            SM,
            pl.BlockSpec((rows, 2 * each), lambda j: (0, j)),
            pl.BlockSpec((rows, d), lambda j: (0, 0)),
        ],
        out_specs=[block, block],
        compiler_params=pltpu.CompilerParams(vmem_limit_bytes=VMEM_LIMIT),
        cost_estimate=TINY,
        name="down_grads",
    )(core, act, og)


def up_grads(core, ren, pg, tab):
    rows, d = ren.shape
    ff = pg.shape[1]
    each = ff // RING
    half = d // 2
    small = tab.shape[0] // (2 * RING)

    def kernel(c, r, g, t, own, other):
        full = tn(r[...], g[...])
        for k in range(2):
            part = full[:, k * each : (k + 1) * each]
            top = jnp.concatenate([part[:half], t[0, k]], axis=0).astype(BF)
            low = jnp.concatenate([part[half:], t[1, k]], axis=0).astype(BF)

            @pl.when(c[4] == 0)
            def _():
                own[k] = top
                other[k] = low

            @pl.when(c[4] != 0)
            def _():
                own[k] = low
                other[k] = top

    shape = jax.ShapeDtypeStruct((RING, half + small, each), BF)
    block = pl.BlockSpec((2, half + small, each), lambda j: (j, 0, 0))
    return pl.pallas_call(
        kernel,
        grid=(RING // 2,),
        out_shape=[shape, shape],
        in_specs=[
            SM,
            pl.BlockSpec((rows, d), lambda j: (0, 0)),
            pl.BlockSpec((rows, 2 * each), lambda j: (0, j)),
            pl.BlockSpec((2, 2, small, each), lambda j: (0, j, 0, 0)),
        ],
        out_specs=[block, block],
        compiler_params=pltpu.CompilerParams(vmem_limit_bytes=VMEM_LIMIT),
        cost_estimate=TINY,
        name="up_grads",
    )(core, ren, pg, tab.reshape(2, RING, small, each))


def ring_plan(count):
    chips = count // 2
    order = [c for c in range(chips) if c % 2 == 0] + [c for c in range(chips) if c % 2 == 1][::-1]
    place = {c: i for i, c in enumerate(order)}
    forward = [(2 * c, 2 * order[(place[c] + 1) % chips]) for c in range(chips)]
    backward = [(2 * c + 1, 2 * order[(place[c] - 1) % chips] + 1) for c in range(chips)]
    return forward + backward


def ring_sums(parts, count, me):
    chips = count // 2
    ring = ring_plan(count)
    swap = [(i, i ^ 1) for i in range(count)]

    def chunk(pair, k):
        return sum(lax.dynamic_index_in_dim(a, k % chips, 0, keepdims=False) for a in pair)

    held = [(own, lax.ppermute(other, "dp", swap)) for own, other in parts]
    moving = [chunk(a, me + chips - 1) for a in held]
    for step in range(chips - 1):
        arrived = [lax.ppermute(c, "dp", ring) for c in moving]
        moving = [r + chunk(a, me + 2 * chips - 2 - step) for r, a in zip(arrived, held)]
    mine, theirs = [[c] for c in moving], [[lax.ppermute(c, "dp", swap)] for c in moving]
    for step in range(chips - 1):
        if step > 0:
            for i, c in enumerate(moving):
                moving[i], theirs[i][-2 if step > 1 else -1] = lax.optimization_barrier(
                    (c, theirs[i][-2 if step > 1 else -1])
                )
        moving = [lax.ppermute(c, "dp", ring) for c in moving]
        for i, c in enumerate(moving):
            mine[i].append(c)
            theirs[i].append(lax.ppermute(c, "dp", swap))
    return mine, theirs


def finish_kernel(p, first, last, threaded, *refs):
    it = iter(refs)
    where = next(it)
    steps = range(first, last)
    chunks = [[{s: next(it) for s in steps} for _ in range(2)] for _ in range(2)]
    for _ in range(threaded):
        next(it)
    down, up, tab_out = next(it), next(it), next(it)
    final = last == RING
    if final:
        fg, fs, tu, tb, td, pb, sg, ss, hb, ob = [next(it) for _ in range(10)]
    taken = [next(it), next(it)]
    given = [next(it), next(it)]
    tab = next(it)
    in_sem, out_sem, tab_sem = next(it), next(it), next(it)
    each = down.shape[1] // RING
    half = down.shape[2] // 2
    small = taken[1].shape[1] - half
    jobs = [(kind, side, s) for s in steps for side in range(2) for kind in range(2)]
    depth = taken[0].shape[0]

    def place(side, s):
        at = where[2 + side] + 2 * RING - s
        return lax.rem(at, RING), (where[4] if side == 0 else 1 - where[4])

    def fetch(n):
        kind, side, s = jobs[n]
        slot = n // 2 % depth
        return pltpu.make_async_copy(chunks[kind][side][s], taken[kind].at[slot], in_sem.at[kind, slot])

    def store(n):
        kind, side, s = jobs[n]
        k, h = place(side, s)
        slot = n // 2 % depth
        by_ff = pl.ds(pl.multiple_of(k * each, each), each)
        by_half = pl.ds(pl.multiple_of(h * half, half), half)
        target = down.at[0, by_ff, by_half] if kind == 0 else up.at[0, by_half, by_ff]
        return pltpu.make_async_copy(given[kind].at[slot], target, out_sem.at[kind, slot])

    def old_table():
        return pltpu.make_async_copy(tab_out, tab, tab_sem)

    lag = 2 * depth
    if first > 0:
        old_table().start()
    for n in range(min(lag, len(jobs))):
        fetch(n).start()
    if first > 0:
        old_table().wait()
    for n, (kind, side, s) in enumerate(jobs):
        fetch(n).wait()
        if n >= lag:
            store(n - lag).wait()
        slot = n // 2 % depth
        given[kind][slot] = taken[kind][slot, 0:half].astype(F32)
        store(n).start()
        if kind == 1:
            k, h = place(side, s)
            tab[pl.ds(pl.multiple_of((h * RING + k) * small, small), small), :] = taken[1][slot, half:].astype(F32)
        if n + lag < len(jobs):
            fetch(n + lag).start()
    keep = pltpu.make_async_copy(tab, tab_out, tab_sem)
    keep.start()

    def vector(ref, row):
        width = tab.shape[1]
        length = ref.shape[1]
        for i in range(-(-length // width)):
            size = min(width, length - i * width)
            ref[:, i * width : i * width + size] = tab[row + i : row + i + 1, 0:size]

    if final:
        tu[:, 0, :] = tab[TU0 : TU0 + p, :]
        td[:, 0, :] = tab[TD0 : TD0 + p, :]
        for ref, row in ((fg, FG0), (fs, FS0), (tb, TB0), (pb, PB0), (sg, SG0), (ss, SS0), (hb, HB0), (ob, OB0)):
            vector(ref, row)
    for n in range(max(0, len(jobs) - lag), len(jobs)):
        store(n).wait()
    keep.wait()


def finish(where, mine, theirs, sizes):
    slots, p, d, ff, th = sizes
    half, each = d // 2, ff // RING
    rows = mine[1][0].shape[0]
    big = [jax.ShapeDtypeStruct(s, F32) for s in ((1, ff, d), (1, d, ff), (TROWS, th))]
    few = [
        jax.ShapeDtypeStruct(s, F32)
        for s in ((1, d), (1, d), (p, 1, th), (1, th), (p, 1, th), (1, p), (1, d), (1, d), (1, ff), (1, d))
    ]
    depth = 4
    scratch = [pltpu.VMEM((depth, half, each), BF), pltpu.VMEM((depth, rows, each), BF)]
    scratch += [pltpu.VMEM((depth, half, each), F32), pltpu.VMEM((depth, half, each), F32)]
    scratch += [
        pltpu.VMEM((TROWS, th), F32), pltpu.SemaphoreType.DMA((2, depth)), pltpu.SemaphoreType.DMA((2, depth)),
        pltpu.SemaphoreType.DMA,
    ]
    results = []
    for first, last in FINISH:
        args = [side[kind][s] for kind in range(2) for side in (mine, theirs) for s in range(first, last)]
        aliases = {1 + len(args) + i: i for i in range(len(results))}
        final = last == RING
        out = pl.pallas_call(
            functools.partial(finish_kernel, p, first, last, len(results)),
            out_shape=big + (few if final else []),
            in_specs=[SM] + [FREE] * len(args) + [ANY] * len(results),
            out_specs=[ANY] * 3 + ([VM] * len(few) if final else []),
            scratch_shapes=scratch,
            input_output_aliases=aliases,
            compiler_params=pltpu.CompilerParams(vmem_limit_bytes=VMEM_LIMIT),
            cost_estimate=pl.CostEstimate(
                flops=1 << 10, bytes_accessed=(last - first) * (4 << 20), transcendentals=0
            ),
            name=f"finish_{first}",
        )(where, *args, *results)
        results = list(out[:3])
    fg, fs, tu, tb, td, pb, sg, ss, hb, ob = out[3:]
    down, up = results[:2]
    return down, up, fg, fs, tu.transpose(1, 0, 2), tb, td.transpose(1, 2, 0), pb, sg, ss, hb, ob


def body(images, cotangent, image_counts, first_gain, first_shift, token_up, token_bias, token_down, patch_bias,
         second_gain, second_shift, channel_up, hidden_bias, channel_down, output_bias):
    slots, p, d = images.shape
    ff, th = channel_up.shape[2], token_up.shape[2]
    sizes = (slots, p, d, ff, th)
    count = lax.axis_size("dp")
    leading = lax.axis_index("section") == 0
    index = lax.axis_index("dp")
    core, chip = index % 2, index // 2
    spot = jnp.where(chip % 2 == 0, chip // 2, count // 2 - 1 - chip // 2)
    turned_spot = count // 2 - 1 - spot
    spots = (jnp.where(core == 0, spot, turned_spot), jnp.where(core == 0, turned_spot, spot))
    sc = jnp.stack([image_counts[0], leading.astype(jnp.int32), *spots, core.astype(jnp.int32)])
    weights = dict(
        g1=first_gain, b1=first_shift, tu=token_up[0], tb=token_bias, tdT=token_down[0].T, pb=patch_bias,
        g2=second_gain, b2=second_shift, w1=channel_up[0], hb=hidden_bias, w2=channel_down[0], ob=output_bias,
    )
    cuts = [(0, 1)] + [(lo, min(2, slots - 1 - lo)) for lo in range(1, slots - 1, 2)] + [(slots - 1, 1)]

    kept, sent, returned = {}, [], []

    def forward(number):
        nonlocal kept
        lo, m = cuts[number]
        kept, out = stage("forward", lo, m, sizes, sc, weights, kept, {"x": images})
        sent.append([lax.ppermute(o, "section", [(0, 1)]) for o in out])

    def both(number):
        nonlocal kept
        lo, m = cuts[number]
        ins = {"x": sent[number], "cot": cotangent}
        kept, grad = stage("both", lo, m, sizes, sc, weights, kept, ins)
        returned.append([lax.ppermute(g, "section", [(1, 0)]) for g in grad])

    def back(numbers):
        nonlocal kept
        lo, m = cuts[numbers[0]][0], sum(cuts[n][1] for n in numbers)
        ins = {"x": images, "cot": [g for n in numbers for g in returned[n]]}
        ins.update({n: kept[n] for n in ("gp", "tgp", "mid", "normed", "tact")})
        kept, _ = stage("back", lo, m, sizes, sc, weights, kept, ins)

    last = len(cuts) - 1
    forward(0)
    forward(1)
    pb, kept["act"] = lax.optimization_barrier((weights["pb"], kept["act"]))
    weights["vec"], weights["tok"] = packed_weights(dict(weights, pb=pb))
    w1, w2, kept["act"] = lax.optimization_barrier((weights["w1"], weights["w2"], kept["act"]))
    weights["w1T"], weights["w2T"] = turned_weights(sc, w1, w2)
    kept["tab"] = jnp.zeros((TROWS, th), F32)
    assert last >= 3
    both(0)
    for number in range(2, last + 1):
        forward(number)
    for number in range(1, last + 1):
        both(number)
        back([number - 1])
    back([last])

    flat = {n: kept[n].reshape(-1, kept[n].shape[-1]) for n in ("act", "ren", "og", "pg")}
    down = down_grads(sc, flat["act"], flat["og"])
    tab = token_grads(sizes, sc, kept)
    up = up_grads(sc, flat["ren"], flat["pg"], tab)
    if count == 2 * RING:
        mine, theirs = ring_sums([down, up], count, spots[0])
        where = sc
    else:
        whole = [jnp.where(core == 0, jnp.stack(pair), jnp.stack(pair[::-1])) for pair in (down, up)]
        whole = [w.astype(BF) for w in lax.psum([w.astype(F32) for w in whole], "dp")]
        mine = [[w[0, -s % RING] for s in range(RING)] for w in whole]
        theirs = [[w[1, -s % RING] for s in range(RING)] for w in whole]
        where = jnp.zeros_like(sc)
    grads = finish(where, mine, theirs, sizes)
    down_sum, up_sum, fg, fs, tu, tb, td, pb, sg, ss, hb, ob = grads
    return (kept["out"][None], kept["ing"][None], fg, fs, tu, tb, td, pb, sg, ss, up_sum, hb, down_sum, ob)


def solution(mesh):
    row = P("section", None)
    mat = P("section", None, None)
    in_specs = (
        P("dp", None, None), P("dp", None, None), P("dp"), row, row, mat, row, mat, row, row, row, mat, row, mat, row,
    )
    stream = P("section", "dp", None, None)
    out_specs = (stream, stream, row, row, mat, row, mat, row, row, row, mat, row, mat, row)
    return jax.shard_map(body, mesh=mesh, in_specs=in_specs, out_specs=out_specs, check_vma=False)
```

```python
import functools
import math

import jax
import jax.numpy as jnp
from jax import lax
from jax.experimental import pallas as pl
from jax.experimental.pallas import tpu as pltpu
from jax.sharding import PartitionSpec as P

EPS = 1e-06
BF, F32 = jnp.bfloat16, jnp.float32
HALF_ROOT = math.sqrt(0.5)
PEAK = 1.0 / math.sqrt(2.0 * math.pi)
FB, BB = 1024, 512
VMEM_LIMIT = 63 << 20
RING = 8
FINISH = ((0, 8),)

ANY = pl.BlockSpec(memory_space=pltpu.HBM)
FREE = pl.BlockSpec(memory_space=pl.ANY)
VM = pl.BlockSpec(memory_space=pltpu.VMEM)
SM = pl.BlockSpec(memory_space=pltpu.SMEM)
TINY = pl.CostEstimate(flops=1 << 10, bytes_accessed=1 << 10, transcendentals=0)

TU0, TD0, FG0, FS0, SG0, SS0, OB0, HB0, TB0, PB0, TROWS = 0, 200, 400, 402, 404, 406, 408, 416, 424, 432, 512

KEPT_FORWARD = ("act", "ren", "normed", "tact", "out", "gp", "tgp", "mid")
KEPT_BOTH = ("act", "ren", "normed", "tact", "out", "og", "pg", "mix", "tpg", "ing", "tab")
KEPT_BACK = ("og", "pg", "ing", "tab")
ZERO_WIDE = ("act", "ren", "og", "pg")
ZERO_OUT = ("out", "ing")


def nn(a, b):
    return jnp.dot(a, b, preferred_element_type=F32)


def nt(a, b):
    return lax.dot_general(a, b, (((1,), (1,)), ((), ())), preferred_element_type=F32)


def tn(a, b):
    return lax.dot_general(a, b, (((0,), (0,)), ((), ())), preferred_element_type=F32)


def padded(rows):
    return -(-rows // 16) * 16


def gelu_parts(z):
    u = z * HALF_ROOT
    phi = 0.5 + 0.5 * lax.erf(u)
    slope = phi + (z * PEAK) * jnp.exp(-(u * u))
    return (z * phi).astype(BF), slope.astype(BF)


def standardize(v):
    center = v - jnp.mean(v, axis=-1, keepdims=True)
    spread = jnp.mean(center * center, axis=-1, keepdims=True)
    inverse = lax.rsqrt(spread + EPS)
    return center * inverse, inverse


def norm_back(y, xhat, inverse):
    return (
        y - jnp.mean(y, axis=-1, keepdims=True) - xhat * jnp.mean(y * xhat, axis=-1, keepdims=True)
    ) * inverse


def rows_sum(v):
    return jnp.sum(v, axis=0, keepdims=True)


def add_row(tab, row, vec):
    width = tab.shape[1]
    for i in range(vec.shape[1] // width):
        tab[row + i : row + i + 1, :] += vec[:, i * width : (i + 1) * width]


def column(row):
    return jnp.transpose(jnp.broadcast_to(row, (8, row.shape[1])))[:, 0:1]


def shapes_of(slots, p, d, ff, th):
    q = padded(p)
    return dict(
        act=((slots, q, ff), BF),
        ren=((slots, q, d), BF),
        og=((slots, q, d), BF),
        pg=((slots, q, ff), BF),
        gp=((slots, p, ff), BF),
        normed=((slots, p, d), BF),
        tact=((slots, th, d), BF),
        tgp=((slots, th, d), BF),
        tpg=((slots, th, d), BF),
        mix=((slots, p, d), BF),
        mid=((slots, p, d), F32),
        out=((slots, p, d), BF),
        ing=((slots, p, d), BF),
        tab=((TROWS, th), F32),
    )


def forward_token(v, x, p, w):
    xh, _ = standardize(x)
    normed = (xh * w["g1"][...] + w["b1"][...]).astype(BF)
    v["normed"][...] = normed
    act, slope = gelu_parts(nn(w["tuT"][...], normed) + column(w["tb"][...]))
    v["tact"][...] = act
    v["tgp"][...] = slope
    v["mid"][...] = x + (nn(w["tdT"][...], act) + column(w["pb"][...]))
    xh2, _ = standardize(v["mid"][...])
    v["ren"][0:p] = (xh2 * w["g2"][...] + w["b2"][...]).astype(BF)


def forward_channel(v, p, w):
    ff = w["w1"].shape[1]
    cuts = [slice(j, j + FB) for j in range(0, ff, FB)]
    pre = nn(v["ren"][0:p], w["w1"][:, cuts[0]])
    total = None
    for j, cut in enumerate(cuts):
        ahead = nn(v["ren"][0:p], w["w1"][:, cuts[j + 1]]) if j + 1 < len(cuts) else None
        if j > 0:
            part = nn(v["act"][0:p, cuts[j - 1]], w["w2"][cuts[j - 1], :])
            total = part if total is None else total + part
        act, slope = gelu_parts(pre + w["hb"][:, cut])
        v["act"][0:p, cut] = act
        v["gp"][:, cut] = slope
        pre = ahead
    total = total + nn(v["act"][0:p, cuts[-1]], w["w2"][cuts[-1], :])
    v["out"][...] = (v["mid"][...] + (total + w["ob"][...])).astype(BF)


def back_slot(v, x, og, p, w, tab, second, wide_done):
    v["og"][0:p] = og
    ff = v["pg"].shape[1]
    width = tab.shape[1]

    def through_down(cut):
        return nn(og, w["w2T"][:, cut]) if "w2T" in w else nt(og, w["w2"][cut, :])

    def through_up(cut):
        pre_grad = v["pg"][0:p, cut]
        return nn(pre_grad, w["w1T"][cut, :]) if "w1T" in w else nt(pre_grad, w["w1"][:, cut])

    cuts = [slice(j, j + BB) for j in range(0, ff, BB)]
    act_grad = through_down(cuts[0])
    norm_grad = None
    for j, cut in enumerate(cuts):
        ahead = through_down(cuts[j + 1]) if j + 1 < len(cuts) else None
        if j > 0:
            if j == 1:
                second()
            part = through_up(cuts[j - 1])
            norm_grad = part if norm_grad is None else norm_grad + part
        pre_grad = act_grad * v["gp"][:, cut].astype(F32)
        v["pg"][0:p, cut] = pre_grad.astype(BF)
        sums = rows_sum(pre_grad)
        for k in range(0, BB, 128):
            c, o = divmod(j * BB + k, width)
            tab[HB0 + c : HB0 + c + 1, o : o + 128] += sums[:, k : k + 128]
        act_grad = ahead
    norm_grad = norm_grad + through_up(cuts[-1])
    wide_done()
    xh2, inv2 = standardize(v["mid"][...])
    live = og.astype(F32)
    add_row(tab, OB0, rows_sum(live))
    add_row(tab, SG0, rows_sum(norm_grad * xh2))
    add_row(tab, SS0, rows_sum(norm_grad))
    middle_grad = live + norm_back(w["g2"][...] * norm_grad, xh2, inv2)
    mix = middle_grad.astype(BF)
    v["mix"][...] = mix
    tpg = (nn(w["td"][...], mix) * v["tgp"][...].astype(F32)).astype(BF)
    v["tpg"][...] = tpg
    first_grad = nn(w["tu"][...], tpg)
    xh, inv = standardize(x)
    add_row(tab, FG0, rows_sum(first_grad * xh))
    add_row(tab, FS0, rows_sum(first_grad))
    v["ing"][...] = (middle_grad + norm_back(w["g1"][...] * first_grad, xh, inv)).astype(BF)


def token_slot(normed, tact, mix, tpg, p, tab):
    ones = jnp.ones((8, mix.shape[-1]), BF)
    tab[TB0 : TB0 + 8, :] += nt(ones, tpg)
    tab[PB0 : PB0 + 8, 0:p] += nt(ones, mix)
    tab[TU0 : TU0 + p, :] += nt(normed, tpg)
    tab[TD0 : TD0 + p, :] += nt(mix, tact)


GROUP_TOKEN = ("normed", "tact", "tgp", "mid", "ren")
GROUP_CHANNEL = ("act", "gp", "out")
GROUP_WIDE = ("og", "pg")
GROUP_BACK = ("mix", "tpg", "ing")


def stage_kernel(plan, *refs):
    mode, lo, m, p = plan["mode"], plan["lo"], plan["m"], plan["p"]
    it = iter(refs)
    sc = next(it)
    ins = {name: [next(it) for _ in range(m if alone else 1)] for name, alone in plan["single"].items()}
    sources = {name: next(it) for name in plan["weights"]}
    for _ in range(plan["threaded"]):
        next(it)
    outs = {name: next(it) for name in plan["outs"]}
    send = [next(it) for _ in range(m)] if plan["send"] else None
    v = {name: next(it) for name in plan["buffers"]}
    tab = next(it) if "tab" in outs else None
    zero, blank_out = (next(it), next(it)) if plan["zeros"] else (None, None)
    w = {name: next(it) for name in plan["weights"]}
    for name in plan["turned"]:
        w[name] = next(it)
    in_sem, out_sem, tab_sem, load_sem = next(it), next(it), next(it), next(it)

    if "vec" in w:
        for row, (name, width) in enumerate(plan["rows"].items()):
            w[name] = w["vec"].at[row : row + 1, 0:width]
        w["tu"], w["tdT"] = w["tok"].at[0], w["tok"].at[1]
    mine = sc[1] == plan["flag"]
    live = jnp.where(mine, jnp.clip(sc[0] - lo, 0, m), 0)
    moved = plan["moved"]

    def load(name):
        return pltpu.make_async_copy(sources[name], w[name], load_sem.at[plan["weights"].index(name)])

    def in_copies(i):
        return [
            pltpu.make_async_copy(
                refs[i] if plan["single"][name] else refs[0].at[lo + i], v[name].at[i], in_sem.at[k, i]
            )
            for k, (name, refs) in enumerate(ins.items())
        ]

    def out_copies(names, i):
        return [
            pltpu.make_async_copy(v[name], outs[name].at[lo + i], out_sem.at[moved.index(name)])
            for name in names
            if name in moved
        ]

    def table(inward):
        rows = slice(FG0, TB0) if mode == "both" else slice(0, TROWS)
        a, b = outs["tab"].at[rows], tab.at[rows]
        return pltpu.make_async_copy(a if inward else b, b if inward else a, tab_sem.at[0])

    def send_copy(i):
        return pltpu.make_async_copy(v[plan["send"]], send[i], out_sem.at[len(moved)])

    def switch(i, action):
        for k in range(m):
            pl.when(i == k)(functools.partial(action, k))

    def zero_copy(name, i):
        source = blank_out if name in ZERO_OUT else zero.at[:, 0 : v[name].shape[-1]]
        return pltpu.make_async_copy(source, outs[name].at[lo + i], tab_sem.at[1])

    def start_all(copies):
        for c in copies:
            c.start()

    def wait_all(copies):
        for c in copies:
            c.wait()

    def first_wait(i, names):
        @pl.when(i == 0)
        def _():
            wait_all([load(name) for name in names])

    def free(i, group):
        @pl.when(i > 0)
        def _():
            wait_all(out_copies(group, i - 1))
            if send is not None and plan["send"] in group:
                send_copy(0).wait()

    blank = jnp.logical_and(mine, live < m)
    if plan["zeros"]:
        @pl.when(blank)
        def _():
            zero[...] = jnp.zeros_like(zero)
            blank_out[...] = jnp.zeros_like(blank_out)
            for i in range(m):
                @pl.when(i >= live)
                def _():
                    start_all([zero_copy(n, i) for n in plan["zeros"]])

    small = [n for n in plan["weights"] if n not in LARGE]

    @pl.when(live > 0)
    def _():
        start_all(in_copies(0))
        for name in plan["weights"]:
            if name in small:
                load(name).start()
        if tab is not None:
            table(True).start()
        for name in ("w1", "w2") if mode != "back" else ("w2", "w1"):
            load(name).start()
        for name in ZERO_WIDE:
            if name in v:
                v[name][p:, :] = jnp.zeros((v[name].shape[0] - p, v[name].shape[1]), BF)
        wait_all([load(name) for name in small])
        for name in plan["turned"]:
            source = {"tuT": "tu", "td": "tdT"}[name]
            w[name][...] = jnp.transpose(w[source][...].astype(F32)).astype(BF)
        if tab is not None:
            table(True).wait()

    def slot(i, carry):
        switch(i, lambda k: wait_all(in_copies(k)))
        for k in range(1, m):
            pl.when(jnp.logical_and(i == k - 1, k < live))(functools.partial(lambda k: start_all(in_copies(k)), k))
        x = v["x"][i].astype(F32)
        cot = v["cot"][i] if mode != "forward" else None
        if mode != "back":
            free(i, GROUP_TOKEN)
            forward_token(v, x, p, w)
            start_all(out_copies(GROUP_TOKEN, i))
            first_wait(i, ("w1", "w2"))
            if mode == "both":
                @pl.when(i == 0)
                def _():
                    start_all([load(n) for n in ("w2T", "w1T")])

            free(i, GROUP_CHANNEL)
            forward_channel(v, p, w)
            if mode == "forward":
                switch(i, lambda k: send_copy(k).start())
            start_all(out_copies(GROUP_CHANNEL, i))
        if mode != "forward":
            first_wait(i, ("w2T", "w1T") if mode == "both" else ("w2",))
            free(i, GROUP_WIDE + GROUP_BACK)
            kept = v if mode == "both" else {**v, **{n: v[n].at[i] for n in ("gp", "tgp", "mid", "normed", "tact")}}
            wide_done = lambda: start_all(out_copies(GROUP_WIDE, i))
            second = lambda: first_wait(i, ("w1",)) if mode == "back" else None
            back_slot(kept, x, cot, p, w, tab, second, wide_done)
            if mode == "both":
                switch(i, lambda k: send_copy(k).start())
            start_all(out_copies(GROUP_BACK, i))
            if mode == "back":
                token_slot(kept["normed"][...], kept["tact"][...], v["mix"][...], v["tpg"][...], p, tab)
        return carry

    lax.fori_loop(0, live, slot, 0)

    @pl.when(live > 0)
    def _():
        if tab is not None:
            table(False).start()
            table(False).wait()
        wait_all(out_copies(GROUP_TOKEN + GROUP_CHANNEL + GROUP_WIDE + GROUP_BACK, live - 1))
        if send is not None:
            send_copy(0).wait()

    if plan["zeros"]:
        @pl.when(blank)
        def _():
            for i in range(m):
                @pl.when(i >= live)
                def _():
                    wait_all([zero_copy(n, i) for n in plan["zeros"]])


ROWS = ("g1", "b1", "g2", "b2", "ob", "hb", "tb", "pb")
LARGE = ("w1", "w2", "w1T", "w2T")


def stage(mode, lo, m, sizes, sc, weights, kept, ins):
    slots, p, d, ff, th = sizes
    shapes = shapes_of(*sizes)
    names = {"forward": KEPT_FORWARD, "both": KEPT_BOTH, "back": KEPT_BACK}[mode]
    moved = [n for n in names if n != "tab"]
    zeros = [n for n in names if n in ZERO_WIDE + ZERO_OUT] if lo + m > 1 else []
    keys = ["vec", "tok"] if "vec" in weights else list(ROWS) + ["tu", "tdT"]
    keys += ["w1", "w2"] + (["w1T", "w2T"] if mode == "both" else [])
    turned = {"forward": ["tuT"], "both": ["tuT", "td"], "back": ["td"]}[mode]
    buffers = {
        "forward": ["x"] + moved,
        "both": ["x", "cot"] + moved + ["gp", "tgp", "mid"],
        "back": ["x", "cot", "gp", "tgp", "mid", "normed", "tact", "mix", "tpg"] + moved,
    }[mode]
    threaded = [n for n in names if n in kept]
    single = {n: isinstance(a, list) for n, a in ins.items()}
    shapes.update(x=((slots, p, d), BF), cot=((slots, p, d), BF))

    given = [a for n, arrays in ins.items() for a in (arrays if single[n] else [arrays])]
    args = [sc] + given + [weights[k] for k in keys]
    specs = [SM] + [FREE if single[n] else ANY for n in ins for _ in range(m if single[n] else 1)] + [ANY] * len(keys)
    aliases = {len(args) + k: names.index(n) for k, n in enumerate(threaded)}
    args += [kept[n] for n in threaded]
    specs += [ANY] * len(threaded)
    out_shape = [jax.ShapeDtypeStruct(*shapes[n]) for n in names]
    send = mode != "back"
    if send:
        out_shape += [jax.ShapeDtypeStruct((p, d), BF)] * m
    scratch = [
        pltpu.VMEM(((m,) if n in ins else ()) + shapes[n][0][1:], shapes[n][1]) for n in buffers
    ]
    if "tab" in names:
        scratch.append(pltpu.VMEM(*shapes["tab"]))
    if zeros:
        scratch += [pltpu.VMEM((padded(p), ff), BF), pltpu.VMEM((p, d), BF)]
    scratch += [pltpu.VMEM(weights[k].shape, weights[k].dtype) for k in keys]
    scratch += [pltpu.VMEM((th, p), BF) for n in turned]
    scratch += [
        pltpu.SemaphoreType.DMA((len(ins), m)),
        pltpu.SemaphoreType.DMA((len(moved) + 1,)),
        pltpu.SemaphoreType.DMA((2,)),
        pltpu.SemaphoreType.DMA((len(keys),)),
    ]
    plan = dict(
        mode=mode, lo=lo, m=m, p=p, flag=0 if mode == "both" else 1, weights=keys,
        threaded=len(threaded), outs=list(names), send={"forward": "out", "both": "ing", "back": None}[mode],
        buffers=buffers, moved=moved, zeros=zeros, turned=turned, single=single, rows=dict(zip(ROWS, (d, d, d, d, d, ff, th, p))),
    )
    outs = pl.pallas_call(
        functools.partial(stage_kernel, plan),
        out_shape=out_shape,
        in_specs=specs,
        out_specs=[ANY] * len(out_shape),
        scratch_shapes=scratch,
        input_output_aliases=aliases,
        compiler_params=pltpu.CompilerParams(vmem_limit_bytes=VMEM_LIMIT),
        cost_estimate=TINY,
        name=f"{mode}_{lo}",
    )(*args)
    new = dict(kept)
    new.update(zip(names, outs))
    return new, (list(outs[-m:]) if send else None)


def token_kernel(p, sc, normed_in, tact_in, mix_in, tpg_in, old, tab_out, normed, tact, mix, tpg, tab, sems, tab_sem):
    live = jnp.where(sc[1] == 0, sc[0], 0)
    pairs = ((normed_in, normed), (tact_in, tact), (mix_in, mix), (tpg_in, tpg))

    def copies(i):
        return [pltpu.make_async_copy(a.at[i], b.at[i], sems.at[k, i]) for k, (a, b) in enumerate(pairs)]

    @pl.when(live > 0)
    def _():
        c = pltpu.make_async_copy(tab_out, tab, tab_sem)
        c.start()

        def begin(i, carry):
            for one in copies(i):
                one.start()
            return carry

        lax.fori_loop(0, live, begin, 0)
        c.wait()

        def work(i, carry):
            for one in copies(i):
                one.wait()
            token_slot(normed[i], tact[i], mix[i], tpg[i], p, tab)
            return carry

        lax.fori_loop(0, live, work, 0)
        c = pltpu.make_async_copy(tab, tab_out, tab_sem)
        c.start()
        c.wait()


def token_grads(sizes, sc, kept):
    slots, p = sizes[:2]
    names = ("normed", "tact", "mix", "tpg")
    shapes = shapes_of(*sizes)
    return pl.pallas_call(
        functools.partial(token_kernel, p),
        out_shape=jax.ShapeDtypeStruct(*shapes["tab"]),
        in_specs=[SM] + [ANY] * 5,
        out_specs=ANY,
        scratch_shapes=[pltpu.VMEM(*shapes[n]) for n in names]
        + [pltpu.VMEM(*shapes["tab"]), pltpu.SemaphoreType.DMA((4, slots)), pltpu.SemaphoreType.DMA],
        input_output_aliases={5: 0},
        compiler_params=pltpu.CompilerParams(vmem_limit_bytes=VMEM_LIMIT),
        cost_estimate=TINY,
        name="token_grads",
    )(sc, *[kept[n] for n in names], kept["tab"])


def packed_weights(weights):
    rows = [weights[n] for n in ROWS]
    pair = [weights["tu"], weights["tdT"]]
    ff = max(r.shape[1] for r in rows)

    given = rows + pair

    def kernel(*refs):
        count = len(given)
        vec, tok = refs[count : count + 2]
        held, sems = refs[count + 2 : -1], refs[-1]
        copies = [pltpu.make_async_copy(a, b, sems.at[k]) for k, (a, b) in enumerate(zip(refs[:count], held))]
        for c in copies:
            c.start()
        vec[...] = jnp.zeros_like(vec)
        for c in copies:
            c.wait()
        for k, r in enumerate(held[: len(rows)]):
            vec[k : k + 1, 0 : r.shape[1]] = r[...]
        for k, r in enumerate(held[len(rows) :]):
            tok[k] = r[...]

    return pl.pallas_call(
        kernel,
        out_shape=[jax.ShapeDtypeStruct((len(rows), ff), F32), jax.ShapeDtypeStruct((2,) + pair[0].shape, BF)],
        in_specs=[ANY] * len(given),
        out_specs=[VM, VM],
        scratch_shapes=[pltpu.VMEM(g.shape, g.dtype) for g in given] + [pltpu.SemaphoreType.DMA((len(given),))],
        compiler_params=pltpu.CompilerParams(vmem_limit_bytes=VMEM_LIMIT),
        cost_estimate=TINY,
        name="packed_weights",
    )(*given)


def turned_kernel(sc, w1, w2, w1T, w2T, a, b, at, bt, in_sem, out_sem):
    ff = w1.shape[1]
    wide = 512
    blocks = ff // wide

    def ins(j):
        cut = pl.ds(j * wide, wide)
        return [
            pltpu.make_async_copy(w1.at[:, cut], a.at[:, cut], in_sem.at[0, j]),
            pltpu.make_async_copy(w2.at[cut], b.at[cut], in_sem.at[1, j]),
        ]

    def outs(j):
        cut = pl.ds(j * wide, wide)
        return [
            pltpu.make_async_copy(at.at[cut], w1T.at[cut], out_sem.at[0, j]),
            pltpu.make_async_copy(bt.at[:, cut], w2T.at[:, cut], out_sem.at[1, j]),
        ]

    @pl.when(sc[1] == 0)
    def _():
        for j in range(blocks):
            for c in ins(j):
                c.start()
        for j in range(blocks):
            for c in ins(j):
                c.wait()
            cut = slice(j * wide, (j + 1) * wide)
            at[cut, :] = jnp.transpose(a[:, cut])
            bt[:, cut] = jnp.transpose(b[cut, :])
            for c in outs(j):
                c.start()
        for j in range(blocks):
            for c in outs(j):
                c.wait()


def turned_weights(sc, w1, w2):
    d, ff = w1.shape
    blocks = ff // 512
    return pl.pallas_call(
        turned_kernel,
        out_shape=[jax.ShapeDtypeStruct((ff, d), BF), jax.ShapeDtypeStruct((d, ff), BF)],
        in_specs=[SM, ANY, ANY],
        out_specs=[ANY, ANY],
        scratch_shapes=[
            pltpu.VMEM((d, ff), BF), pltpu.VMEM((ff, d), BF), pltpu.VMEM((ff, d), BF), pltpu.VMEM((d, ff), BF),
            pltpu.SemaphoreType.DMA((2, blocks)), pltpu.SemaphoreType.DMA((2, blocks)),
        ],
        compiler_params=pltpu.CompilerParams(vmem_limit_bytes=VMEM_LIMIT),
        cost_estimate=TINY,
        name="turned_weights",
    )(sc, w1, w2)


def split_halves(core, full, own, other):
    half = full.shape[1] // 2
    left, right = full[:, :half].astype(BF), full[:, half:].astype(BF)

    @pl.when(core == 0)
    def _():
        own[...] = left
        other[...] = right

    @pl.when(core != 0)
    def _():
        own[...] = right
        other[...] = left


def down_grads(core, act, og):
    rows, ff = act.shape
    d = og.shape[1]
    each = ff // RING

    def kernel(c, a, g, own, other):
        full = tn(a[...], g[...])
        for k in range(2):
            split_halves(c[4], full[k * each : (k + 1) * each], own.at[k], other.at[k])

    shape = jax.ShapeDtypeStruct((RING, each, d // 2), BF)
    block = pl.BlockSpec((2, each, d // 2), lambda j: (j, 0, 0))
    return pl.pallas_call(
        kernel,
        grid=(RING // 2,),
        out_shape=[shape, shape],
        in_specs=[
            SM,
            pl.BlockSpec((rows, 2 * each), lambda j: (0, j)),
            pl.BlockSpec((rows, d), lambda j: (0, 0)),
        ],
        out_specs=[block, block],
        compiler_params=pltpu.CompilerParams(vmem_limit_bytes=VMEM_LIMIT),
        cost_estimate=TINY,
        name="down_grads",
    )(core, act, og)


def up_grads(core, ren, pg, tab):
    rows, d = ren.shape
    ff = pg.shape[1]
    each = ff // RING
    half = d // 2
    small = tab.shape[0] // (2 * RING)

    def kernel(c, r, g, t, own, other):
        full = tn(r[...], g[...])
        for k in range(2):
            part = full[:, k * each : (k + 1) * each]
            top = jnp.concatenate([part[:half], t[0, k]], axis=0).astype(BF)
            low = jnp.concatenate([part[half:], t[1, k]], axis=0).astype(BF)

            @pl.when(c[4] == 0)
            def _():
                own[k] = top
                other[k] = low

            @pl.when(c[4] != 0)
            def _():
                own[k] = low
                other[k] = top

    shape = jax.ShapeDtypeStruct((RING, half + small, each), BF)
    block = pl.BlockSpec((2, half + small, each), lambda j: (j, 0, 0))
    return pl.pallas_call(
        kernel,
        grid=(RING // 2,),
        out_shape=[shape, shape],
        in_specs=[
            SM,
            pl.BlockSpec((rows, d), lambda j: (0, 0)),
            pl.BlockSpec((rows, 2 * each), lambda j: (0, j)),
            pl.BlockSpec((2, 2, small, each), lambda j: (0, j, 0, 0)),
        ],
        out_specs=[block, block],
        compiler_params=pltpu.CompilerParams(vmem_limit_bytes=VMEM_LIMIT),
        cost_estimate=TINY,
        name="up_grads",
    )(core, ren, pg, tab.reshape(2, RING, small, each))


def ring_plan(count):
    chips = count // 2
    order = [c for c in range(chips) if c % 2 == 0] + [c for c in range(chips) if c % 2 == 1][::-1]
    place = {c: i for i, c in enumerate(order)}
    forward = [(2 * c, 2 * order[(place[c] + 1) % chips]) for c in range(chips)]
    backward = [(2 * c + 1, 2 * order[(place[c] - 1) % chips] + 1) for c in range(chips)]
    return forward + backward


def ring_sums(parts, count, me):
    chips = count // 2
    ring = ring_plan(count)
    swap = [(i, i ^ 1) for i in range(count)]

    def chunk(pair, k):
        return sum(lax.dynamic_index_in_dim(a, k % chips, 0, keepdims=False) for a in pair)

    held = [(own, lax.ppermute(other, "dp", swap)) for own, other in parts]
    moving = [chunk(a, me + chips - 1) for a in held]
    for step in range(chips - 1):
        arrived = [lax.ppermute(c, "dp", ring) for c in moving]
        moving = [r + chunk(a, me + 2 * chips - 2 - step) for r, a in zip(arrived, held)]
    mine, theirs = [[c] for c in moving], [[lax.ppermute(c, "dp", swap)] for c in moving]
    for step in range(chips - 1):
        if step > 0:
            for i, c in enumerate(moving):
                moving[i], theirs[i][-2 if step > 1 else -1] = lax.optimization_barrier(
                    (c, theirs[i][-2 if step > 1 else -1])
                )
        moving = [lax.ppermute(c, "dp", ring) for c in moving]
        for i, c in enumerate(moving):
            mine[i].append(c)
            theirs[i].append(lax.ppermute(c, "dp", swap))
    return mine, theirs


def finish_kernel(p, first, last, threaded, *refs):
    it = iter(refs)
    where = next(it)
    steps = range(first, last)
    chunks = [[{s: next(it) for s in steps} for _ in range(2)] for _ in range(2)]
    for _ in range(threaded):
        next(it)
    down, up, tab_out = next(it), next(it), next(it)
    final = last == RING
    if final:
        fg, fs, tu, tb, td, pb, sg, ss, hb, ob = [next(it) for _ in range(10)]
    taken = [next(it), next(it)]
    given = [next(it), next(it)]
    tab = next(it)
    in_sem, out_sem, tab_sem = next(it), next(it), next(it)
    each = down.shape[1] // RING
    half = down.shape[2] // 2
    small = taken[1].shape[1] - half
    jobs = [(kind, side, s) for s in steps for side in range(2) for kind in range(2)]
    depth = taken[0].shape[0]

    def place(side, s):
        at = where[2 + side] + 2 * RING - s
        return lax.rem(at, RING), (where[4] if side == 0 else 1 - where[4])

    def fetch(n):
        kind, side, s = jobs[n]
        slot = n // 2 % depth
        return pltpu.make_async_copy(chunks[kind][side][s], taken[kind].at[slot], in_sem.at[kind, slot])

    def store(n):
        kind, side, s = jobs[n]
        k, h = place(side, s)
        slot = n // 2 % depth
        by_ff = pl.ds(pl.multiple_of(k * each, each), each)
        by_half = pl.ds(pl.multiple_of(h * half, half), half)
        target = down.at[0, by_ff, by_half] if kind == 0 else up.at[0, by_half, by_ff]
        return pltpu.make_async_copy(given[kind].at[slot], target, out_sem.at[kind, slot])

    def old_table():
        return pltpu.make_async_copy(tab_out, tab, tab_sem)

    lag = 2 * depth
    if first > 0:
        old_table().start()
    for n in range(min(lag, len(jobs))):
        fetch(n).start()
    if first > 0:
        old_table().wait()
    for n, (kind, side, s) in enumerate(jobs):
        fetch(n).wait()
        if n >= lag:
            store(n - lag).wait()
        slot = n // 2 % depth
        given[kind][slot] = taken[kind][slot, 0:half].astype(F32)
        store(n).start()
        if kind == 1:
            k, h = place(side, s)
            tab[pl.ds(pl.multiple_of((h * RING + k) * small, small), small), :] = taken[1][slot, half:].astype(F32)
        if n + lag < len(jobs):
            fetch(n + lag).start()
    keep = pltpu.make_async_copy(tab, tab_out, tab_sem)
    keep.start()

    def vector(ref, row):
        width = tab.shape[1]
        length = ref.shape[1]
        for i in range(-(-length // width)):
            size = min(width, length - i * width)
            ref[:, i * width : i * width + size] = tab[row + i : row + i + 1, 0:size]

    if final:
        tu[:, 0, :] = tab[TU0 : TU0 + p, :]
        td[:, 0, :] = tab[TD0 : TD0 + p, :]
        for ref, row in ((fg, FG0), (fs, FS0), (tb, TB0), (pb, PB0), (sg, SG0), (ss, SS0), (hb, HB0), (ob, OB0)):
            vector(ref, row)
    for n in range(max(0, len(jobs) - lag), len(jobs)):
        store(n).wait()
    keep.wait()


def finish(where, mine, theirs, sizes):
    slots, p, d, ff, th = sizes
    half, each = d // 2, ff // RING
    rows = mine[1][0].shape[0]
    big = [jax.ShapeDtypeStruct(s, F32) for s in ((1, ff, d), (1, d, ff), (TROWS, th))]
    few = [
        jax.ShapeDtypeStruct(s, F32)
        for s in ((1, d), (1, d), (p, 1, th), (1, th), (p, 1, th), (1, p), (1, d), (1, d), (1, ff), (1, d))
    ]
    depth = 8
    scratch = [pltpu.VMEM((depth, half, each), BF), pltpu.VMEM((depth, rows, each), BF)]
    scratch += [pltpu.VMEM((depth, half, each), F32), pltpu.VMEM((depth, half, each), F32)]
    scratch += [
        pltpu.VMEM((TROWS, th), F32), pltpu.SemaphoreType.DMA((2, depth)), pltpu.SemaphoreType.DMA((2, depth)),
        pltpu.SemaphoreType.DMA,
    ]
    results = []
    for first, last in FINISH:
        args = [side[kind][s] for kind in range(2) for side in (mine, theirs) for s in range(first, last)]
        aliases = {1 + len(args) + i: i for i in range(len(results))}
        final = last == RING
        out = pl.pallas_call(
            functools.partial(finish_kernel, p, first, last, len(results)),
            out_shape=big + (few if final else []),
            in_specs=[SM] + [FREE] * len(args) + [ANY] * len(results),
            out_specs=[ANY] * 3 + ([VM] * len(few) if final else []),
            scratch_shapes=scratch,
            input_output_aliases=aliases,
            compiler_params=pltpu.CompilerParams(vmem_limit_bytes=VMEM_LIMIT),
            cost_estimate=pl.CostEstimate(
                flops=1 << 10, bytes_accessed=(last - first) * (4 << 20), transcendentals=0
            ),
            name=f"finish_{first}",
        )(where, *args, *results)
        results = list(out[:3])
    fg, fs, tu, tb, td, pb, sg, ss, hb, ob = out[3:]
    down, up = results[:2]
    return down, up, fg, fs, tu.transpose(1, 0, 2), tb, td.transpose(1, 2, 0), pb, sg, ss, hb, ob


def body(images, cotangent, image_counts, first_gain, first_shift, token_up, token_bias, token_down, patch_bias,
         second_gain, second_shift, channel_up, hidden_bias, channel_down, output_bias):
    slots, p, d = images.shape
    ff, th = channel_up.shape[2], token_up.shape[2]
    sizes = (slots, p, d, ff, th)
    count = lax.axis_size("dp")
    leading = lax.axis_index("section") == 0
    index = lax.axis_index("dp")
    core, chip = index % 2, index // 2
    spot = jnp.where(chip % 2 == 0, chip // 2, count // 2 - 1 - chip // 2)
    turned_spot = count // 2 - 1 - spot
    spots = (jnp.where(core == 0, spot, turned_spot), jnp.where(core == 0, turned_spot, spot))
    sc = jnp.stack([image_counts[0], leading.astype(jnp.int32), *spots, core.astype(jnp.int32)])
    weights = dict(
        g1=first_gain, b1=first_shift, tu=token_up[0], tb=token_bias, tdT=token_down[0].T, pb=patch_bias,
        g2=second_gain, b2=second_shift, w1=channel_up[0], hb=hidden_bias, w2=channel_down[0], ob=output_bias,
    )
    cuts = [(0, 1)] + [(lo, min(2, slots - 1 - lo)) for lo in range(1, slots - 1, 2)] + [(slots - 1, 1)]

    kept, sent, returned = {}, [], []

    def forward(number):
        nonlocal kept
        lo, m = cuts[number]
        kept, out = stage("forward", lo, m, sizes, sc, weights, kept, {"x": images})
        sent.append([lax.ppermute(o, "section", [(0, 1)]) for o in out])

    def both(number):
        nonlocal kept
        lo, m = cuts[number]
        ins = {"x": sent[number], "cot": cotangent}
        kept, grad = stage("both", lo, m, sizes, sc, weights, kept, ins)
        returned.append([lax.ppermute(g, "section", [(1, 0)]) for g in grad])

    def back(numbers):
        nonlocal kept
        lo, m = cuts[numbers[0]][0], sum(cuts[n][1] for n in numbers)
        ins = {"x": images, "cot": [g for n in numbers for g in returned[n]]}
        ins.update({n: kept[n] for n in ("gp", "tgp", "mid", "normed", "tact")})
        kept, _ = stage("back", lo, m, sizes, sc, weights, kept, ins)

    last = len(cuts) - 1
    forward(0)
    forward(1)
    pb, kept["act"] = lax.optimization_barrier((weights["pb"], kept["act"]))
    weights["vec"], weights["tok"] = packed_weights(dict(weights, pb=pb))
    w1, w2, kept["act"] = lax.optimization_barrier((weights["w1"], weights["w2"], kept["act"]))
    weights["w1T"], weights["w2T"] = turned_weights(sc, w1, w2)
    kept["tab"] = jnp.zeros((TROWS, th), F32)
    assert last >= 3
    both(0)
    for number in range(2, last + 1):
        forward(number)
    for number in range(1, last + 1):
        both(number)
        back([number - 1])
    back([last])

    flat = {n: kept[n].reshape(-1, kept[n].shape[-1]) for n in ("act", "ren", "og", "pg")}
    down = down_grads(sc, flat["act"], flat["og"])
    tab = token_grads(sizes, sc, kept)
    up = up_grads(sc, flat["ren"], flat["pg"], tab)
    if count == 2 * RING:
        mine, theirs = ring_sums([down, up], count, spots[0])
        where = sc
    else:
        whole = [jnp.where(core == 0, jnp.stack(pair), jnp.stack(pair[::-1])) for pair in (down, up)]
        whole = [w.astype(BF) for w in lax.psum([w.astype(F32) for w in whole], "dp")]
        mine = [[w[0, -s % RING] for s in range(RING)] for w in whole]
        theirs = [[w[1, -s % RING] for s in range(RING)] for w in whole]
        where = jnp.zeros_like(sc)
    grads = finish(where, mine, theirs, sizes)
    down_sum, up_sum, fg, fs, tu, tb, td, pb, sg, ss, hb, ob = grads
    return (kept["out"][None], kept["ing"][None], fg, fs, tu, tb, td, pb, sg, ss, up_sum, hb, down_sum, ob)


def solution(mesh):
    row = P("section", None)
    mat = P("section", None, None)
    in_specs = (
        P("dp", None, None), P("dp", None, None), P("dp"), row, row, mat, row, mat, row, row, row, mat, row, mat, row,
    )
    stream = P("section", "dp", None, None)
    out_specs = (stream, stream, row, row, mat, row, mat, row, row, row, mat, row, mat, row)
    return jax.shard_map(body, mesh=mesh, in_specs=in_specs, out_specs=out_specs, check_vma=False)
```
